512 devices in a mesh: expert: 64 (over z, y), tensor: 4 (over x), dp: 2 (over core).
Axes of the slice: x: 4, y: 8, z: 8, core: 2. Of those that a mesh axis runs over, the one named last changes fastest.
Arguments:
- tokens: bfloat16 [4096, 3584], P(('dp', 'expert'), 'tensor'), parts along dimension 0, may hold values from -6 to 6
- dither: int32 [4096], P(('dp', 'expert')), parts along dimension 0, may hold values from 0 to 255
- expert_ids: int32 [4096, 8], P(('dp', 'expert')), parts along dimension 0, may hold values from 0 to 31, all different within a row; in each aligned block of 32 rows (0 to 31, 32 to 63, ...) at most 16 rows name the same one
- gate_values: float32 [4096, 8], P(('dp', 'expert')), parts along dimension 0, may hold values from 0.05 to 0.5
- gate_weight: bfloat16 [64, 3584, 512], P('expert', None, 'tensor'), may hold values from -0.09375 to 0.09375
- up_weight: bfloat16 [64, 3584, 512], P('expert', None, 'tensor'), may hold values from -0.09375 to 0.09375
- down_weight: bfloat16 [64, 512, 3584], P('expert', None, 'tensor'), may hold values from -0.1875 to 0.1875
Outputs:
- moe_output: bfloat16 [4096, 3584], P(('dp', 'expert'), 'tensor'), parts along dimension 0
The draws below stay inside these ranges and needn't reach their ends.
There are 2 independent parts, one for each index of `dp`. The reference program is written for one: setup_inputs(seed, part) draws one part's arguments, and reference() takes and returns one part's arrays. A program takes and returns all parts, laid end to end along the dimension named above; an argument that names none is the same for every part. Nothing has to cross between parts.
Inputs may be any that keep to these rules, and one draw needn't show every extreme that they name: `expert_ids`: each row names 8 different experts. Among the 32 rows of one index of the expert axis no expert is named more than 16 times, a bound that some block reaches.
All inputs are finite; a program needn't handle non-finite values.
Results may differ from the reference program's by a relative error of at most 0.0057.
Values may be sent and summed in bfloat16 or wider, within the bound.
A program may use at most 64 MiB of HBM per device.

```python
import math
import jax
import jax.numpy as jnp
import numpy as np
from jax import lax

D = 3584
FF = 1024
TOK_E = 32
EXPERTS = 32
TOPK = 8
CAP = 16
TOKENS = 2048
N_EXPERT = 64


def touch_ends(drawn, key, least, largest):
    extent = drawn.shape
    place = [jax.random.randint(jax.random.fold_in(key, axis), (), 0, extent[axis]) for axis in range(len(extent))]
    drawn = drawn.at[tuple(place)].set(least)
    longest = extent.index(max(extent))
    place[longest] = (place[longest] + 1) % extent[longest]
    return drawn.at[tuple(place)].set(largest)


def block_levels(stream_key, shape, shards, low, largest):
    def one(axis_at, parts):
        heights = jax.random.uniform(jax.random.fold_in(jax.random.fold_in(stream_key, 6), axis_at), (parts,), jnp.float32, low / len(shards), largest / len(shards))
        return jnp.repeat(jnp.exp(heights), shape[axis_at] // parts).reshape((-1,) + (1,) * (len(shape) - axis_at - 1))

    factor_of = one(*shards[0])
    for cut in shards[1:]:
        factor_of = factor_of * one(*cut)
    return factor_of


def shared_out(rng, own, number, rows, count, top, reach, lean):
    ranking = jax.random.permutation(rng, count)
    packed, ordinary = load_shares(count, rows * top, reach, lean, True), load_shares(count, rows * top, reach, lean, False)
    places = jnp.arange(count)

    def named(tallies, offset_by):
        used = int((tallies > 0).sum())
        fixed = max(1, used // 4)
        passed = fixed + (places - fixed + offset_by * (used - fixed)) % max(1, count - fixed)
        return jnp.zeros((count,), jnp.int32).at[ranking[jnp.where(places < fixed, places, passed)]].set(jnp.asarray(tallies, jnp.int32))

    tallies = jnp.where(number % 4 == 0, named(packed, number // 4), named(ordinary, number - number // 4 - 1))
    mixed = jax.random.permutation(jax.random.fold_in(own, 3), count)
    source_of, taker = mixed[0:count // 2 * 2:2], mixed[1:count // 2 * 2:2]
    room = jnp.minimum(tallies[source_of] - 1, reach - tallies[taker]) // 2
    room = jnp.where((source_of == ranking[0]) | (taker == ranking[0]) | (tallies[taker] == 0), 0, jnp.maximum(room, 0))
    passed = jax.random.randint(jax.random.fold_in(own, 4), (count // 2,), 0, 1 << 20) % (room + 1)
    tallies = tallies.at[source_of].add(-passed).at[taker].add(passed)
    items = jnp.searchsorted(jnp.cumsum(tallies), jnp.arange(rows * top), side="right").astype(jnp.int32)
    table = items.reshape(top, rows).T
    table = table[jax.random.permutation(jax.random.fold_in(own, 1), rows)]
    offset_by = jax.random.randint(jax.random.fold_in(own, 2), (rows, 1), 0, top)
    return jnp.take_along_axis(table, (jnp.arange(top)[None, :] + offset_by) % top, axis=1)


def load_shares(number_of, total, limit, slope, full):
    loads = [(1 << 20) // math.isqrt(standing ** slope) + 1 for standing in range(1, number_of + 1)]
    largest = limit if full else min(limit, max(-(-total // number_of), total * loads[0] // sum(loads)))
    least = 1 if total - largest >= number_of - 1 else 0
    counts, spare = [largest] + [least] * (number_of - 1), total - largest - least * (number_of - 1)
    while spare > 0:
        movable = [i for i in range(1, number_of) if counts[i] < largest] or [i for i in range(1, number_of) if counts[i] < limit]
        whole, budget = sum([loads[i] for i in movable]), spare
        for i in movable:
            extra = min(limit - counts[i], max(1, budget * loads[i] // whole), spare)
            counts[i] = counts[i] + extra
            spare = spare - extra
    return np.array(counts)


def centred(rng, shape, scale, most, cuts=(), kind=jnp.bfloat16):
    entries = jax.random.normal(rng, shape, jnp.float32) * scale
    if len(cuts) > 0:
        entries = block_levels(rng, shape, cuts, -0.22, 0.18) * entries
    return jnp.clip(entries, min=-most, max=most).astype(kind)


def setup_inputs(seed: int = 0, part: int = 0) -> dict:
    arg_keys = jax.random.split(jax.random.key(seed), 8)
    part_keys = jax.random.split(jax.random.fold_in(arg_keys[7], part), 8)
    tokens = centred(part_keys[0], (TOKENS, D), 1.0, 6.0, ((0, 64), (1, 4)))
    dither = touch_ends(jax.random.randint(part_keys[1], (TOKENS,), 0, 256), jax.random.fold_in(part_keys[1], 1), 0, 255).astype(jnp.int32)
    expert_ids_keys = jax.random.split(jax.random.fold_in(part_keys[2], 1), TOKENS // TOK_E)
    expert_ids_turns = jax.random.permutation(jax.random.fold_in(part_keys[2], 3), TOKENS // TOK_E)
    expert_ids = jax.vmap(lambda own, number: shared_out(jax.random.fold_in(part_keys[2], 2), own, number, TOK_E, EXPERTS, TOPK, CAP, 2))(expert_ids_keys, expert_ids_turns).reshape((TOKENS, TOPK))
    gate_values = jnp.clip(jnp.exp(math.log(0.5) - 2.3025851 * jax.random.uniform(part_keys[3], (TOKENS, TOPK), jnp.float32) ** block_levels(part_keys[3], (TOKENS, TOPK), ((0, 64),), -0.2, 0.2)), 0.05, 0.5)
    gate_weight = centred(arg_keys[4], (2 * EXPERTS, D, FF // 2), D ** -0.5, 0.09375, ((0, 64), (2, 4)))
    up_weight = centred(arg_keys[5], (2 * EXPERTS, D, FF // 2), D ** -0.5, 0.09375, ((0, 64), (2, 4)))
    down_weight = centred(arg_keys[6], (2 * EXPERTS, FF // 2, D), FF ** -0.5, 0.1875, ((0, 64), (2, 4)))
    return dict(tokens=tokens, dither=dither, expert_ids=expert_ids, gate_values=gate_values, gate_weight=gate_weight, up_weight=up_weight, down_weight=down_weight)


def dither_round(values, dither, column_start):
    scaled = values.astype(jnp.float32)
    magnitude = jnp.abs(scaled)
    grid_step = jnp.full_like(scaled, 2.0 ** -26)
    for octave in range(-23, 4):
        grid_step = grid_step + jnp.where(magnitude >= 2.0 ** octave, 2.0 ** (octave - 3), 0.0)
    columns = column_start + jnp.arange(scaled.shape[1], dtype=jnp.int32)
    offset = (dither[:, None] + 97 * columns[None, :]) % 256
    jitter = (offset.astype(jnp.float32) + 0.5) / 256.0
    return (jnp.floor(scaled / grid_step + jitter) * grid_step).astype(jnp.bfloat16)


def reference(tokens, dither, expert_ids, gate_values, gate_weight, up_weight, down_weight):
    rounded = dither_round(tokens, dither, 0)
    block_ids = expert_ids.reshape(N_EXPERT, TOK_E * TOPK)
    onehot = (block_ids[:, :, None] == jnp.arange(EXPERTS, dtype=jnp.int32)[None, None, :]).astype(jnp.int32)
    before = jnp.cumsum(onehot, axis=1) - onehot
    slot_index = jnp.sum(before * onehot, axis=2)
    source = jnp.arange(N_EXPERT, dtype=jnp.int32)[:, None]
    position = (source * CAP + slot_index).reshape(-1).astype(jnp.int32)
    flat_ids = expert_ids.reshape(-1).astype(jnp.int32)
    token_index = jnp.arange(TOKENS * TOPK, dtype=jnp.int32) // TOPK
    buffers = jnp.zeros((EXPERTS, N_EXPERT * CAP, D), jnp.bfloat16)
    buffers = buffers.at[flat_ids, position].set(rounded[token_index])
    gate_full = jnp.transpose(gate_weight.reshape(EXPERTS, 2, D, FF // 2), (0, 2, 1, 3)).reshape(EXPERTS, D, FF)
    up_full = jnp.transpose(up_weight.reshape(EXPERTS, 2, D, FF // 2), (0, 2, 1, 3)).reshape(EXPERTS, D, FF)
    down_full = down_weight.reshape(EXPERTS, 2, FF // 2, D)

    def expert_apply(operands):
        rows_in, gate_mat, up_mat, down_mat = operands
        gate_pre = jnp.dot(rows_in, gate_mat, preferred_element_type=jnp.float32)
        up_pre = jnp.dot(rows_in, up_mat, preferred_element_type=jnp.float32)
        hidden = (jax.nn.silu(gate_pre) * up_pre).astype(jnp.bfloat16)
        halves = jnp.einsum(
            "rpf,pfd->prd",
            hidden.reshape(-1, 2, FF // 2).astype(jnp.float32),
            down_mat.astype(jnp.float32),
        )
        rounded_parts = lax.optimization_barrier(halves.astype(jnp.bfloat16))
        return jnp.sum(rounded_parts.astype(jnp.float32), axis=0)

    outputs = lax.map(expert_apply, (buffers, gate_full, up_full, down_full))
    picked = outputs[flat_ids, position].reshape(TOKENS, TOPK, D)
    token_mix = jnp.sum(gate_values[:, :, None] * picked, axis=1)
    return token_mix.astype(jnp.bfloat16)
```

```python
import functools

import jax
import jax.numpy as jnp
from jax import lax
from jax.experimental import pallas as pl
from jax.experimental.pallas import tpu as pltpu
from jax.sharding import PartitionSpec as P

MESH = pl.DeviceIdType.MESH
BF = jnp.bfloat16
F32 = jnp.float32
N = 8
X = 4
HALF = 16
GROUPS = 8
CUT = 512


def iota(shape, axis):
    return lax.broadcasted_iota(jnp.int32, shape, axis)


def dither_round(values, dither_row, column_start):
    rows, cols = values.shape
    scaled = values.astype(F32)
    magnitude = jnp.abs(scaled)
    grid = jnp.full_like(scaled, 2.0**-26)
    inverse = jnp.full_like(scaled, 2.0**26)
    for octave in range(-23, 4):
        above = magnitude >= 2.0**octave
        grid = jnp.where(above, 2.0 ** (octave - 2), grid)
        inverse = jnp.where(above, 2.0 ** (2 - octave), inverse)
    square = jnp.broadcast_to(dither_row.astype(F32), (rows, rows))
    diagonal = iota((rows, rows), 0) == iota((rows, rows), 1)
    column = jnp.sum(jnp.where(diagonal, square, 0.0), axis=1, keepdims=True).astype(jnp.int32)
    offset = (column + 97 * (column_start + iota((rows, cols), 1))) & 255
    jitter = (offset.astype(F32) + 0.5) / 256.0
    return (jnp.floor(scaled * inverse + jitter) * grid).astype(BF)


def gate_table(ids, gates):
    rows = []
    lane = iota((HALF, 128), 1)
    own = lane % HALF == iota((HALF, 128), 0)
    for r in range(8):
        part = slice((r // 4) * HALF, (r // 4) * HALF + HALF)
        expert = (r % 4) * 8 + lane // HALF
        total = jnp.zeros((HALF, 128), F32)
        for k in range(ids.shape[1]):
            total = total + jnp.where(ids[part, k : k + 1] == expert, gates[part, k : k + 1], 0.0)
        rows.append(jnp.sum(jnp.where(own, total, 0.0), axis=0, keepdims=True))
    return jnp.concatenate(rows, axis=0)


def group_of(n):
    return jnp.where(n % 2 == 1, 4 - (n + 1) // 2, 4 + n // 2)


def kernel(
    tok, dit, ids, gat, gw, uw, dw, out,
    XA, XB, AUX, WX, WF, WD, PT, GS, OWN, NB, SX, T1, R2, HB, CA, RA, CB, RB, FA, FB, SA, SB, TA, TB,
    ag_s, ag_r, w_s, w_r, w_l, x_s, x_r, ra_s, ra_r, b_s, b_r, fa_s, fa_r, fb_s, fb_r,
):
    here = lax.axis_index("expert")
    t = lax.axis_index("tensor")
    c = lax.axis_index("dp")
    y, z = here % N, here // N
    e = here // 2

    def ydev(k):
        return {"expert": z * N + (y + k + N) % N}

    def zdev(k):
        return {"expert": ((z + k + N) % N) * N + y}

    def xdev(k):
        return {"tensor": (t + k + X) % X}

    def copy(src, dst, ss, rs, dev):
        return pltpu.make_async_remote_copy(
            src_ref=src, dst_ref=dst, send_sem=ss, recv_sem=rs, device_id=dev, device_id_type=MESH
        )

    barrier = pltpu.get_barrier_semaphore()
    peers = [ydev(k) for k in range(1, N)] + [zdev(k) for k in range(1, N)]
    peers += [xdev(1), xdev(-1), {"dp": 1 - c}]
    for peer in peers:
        pl.semaphore_signal(barrier, inc=1, device_id=peer, device_id_type=MESH)

    local = [
        pltpu.make_async_copy(dw.at[0], WD, w_l.at[0]),
        pltpu.make_async_copy(gw.at[0, pl.ds(pl.multiple_of(t * 896, 128), 896)], WX.at[0, :, 0:128], w_l.at[1]),
        pltpu.make_async_copy(uw.at[0, pl.ds(pl.multiple_of(t * 896, 128), 896)], WX.at[0, :, 128:256], w_l.at[2]),
    ]
    for d in local:
        d.start()

    block = dither_round(tok[...], dit[...], t * tok.shape[1])
    XA[0, 0] = block[:HALF]
    XB[0, 0] = block[HALF:]
    AUX[0, 0] = gate_table(ids[...], gat[...])
    pl.semaphore_wait(barrier, len(peers))

    sent = []
    counter = [0]

    def go(src, dst, rs, dev):
        d = copy(src, dst, ag_s.at[counter[0]], ag_r.at[rs], dev)
        counter[0] += 1
        d.start()
        sent.append(d)

    def landed(ref, rs):
        pltpu.make_async_copy(ref, ref, ag_r.at[rs]).wait()

    A1, U1, B1 = 0, 8, 16
    A2, B2, U2 = 24, 40, 56

    def first_hop(k):
        h = k // 4
        go(XA.at[0, k], XA.at[1, k], A2 + 2 + h, zdev(1))
        go(XA.at[0, k], XA.at[7, k], A2 + 14 + h, zdev(-1))
        go(XB.at[0, k], XB.at[1, k], B2 + 2 + h, ydev(1))
        go(XB.at[0, k], XB.at[7, k], B2 + 14 + h, ydev(-1))

    def small(src, dst, sign):
        go(XA.at[0, src], XA.at[0, dst], A1 + dst, ydev(sign))
        go(AUX.at[0, src], AUX.at[0, dst], U1 + dst, ydev(sign))
        go(XB.at[0, src], XB.at[0, dst], B1 + dst, zdev(sign))

    def small_landed(k):
        landed(XA.at[0, k], A1 + k)
        landed(AUX.at[0, k], U1 + k)
        landed(XB.at[0, k], B1 + k)

    small(0, 1, 1)
    small(0, 7, -1)
    first_hop(0)

    half = pl.multiple_of(c * 448, 64)
    wide = (slice(0, 128), slice(128, 256))

    def rows_for(k, start, size):
        return pl.ds(pl.multiple_of(((t + k + X) % X) * 896 + c * 448 + start, 32), size)

    near, far = [], []
    for p, w in enumerate((gw, uw)):
        near.append(copy(w.at[0, rows_for(1, 0, 448)], WX.at[3, pl.ds(half, 448), wide[p]], w_s.at[p], w_r.at[p], xdev(1)))
        near.append(copy(w.at[0, rows_for(-1, 0, 448)], WX.at[1, pl.ds(half, 448), wide[p]], w_s.at[2 + p], w_r.at[2 + p], xdev(-1)))
        far.append(copy(w.at[0, rows_for(2, 0, 224)], WF.at[0, :, wide[p]], w_s.at[4 + p], w_r.at[4 + p], xdev(1)))
        far.append(copy(w.at[0, rows_for(2, 224, 224)], WF.at[1, :, wide[p]], w_s.at[6 + p], w_r.at[6 + p], xdev(-1)))
    for d in far + near:
        d.start()
    lower = pl.ds(pl.multiple_of(c * 448, 32), 224)
    upper = pl.ds(pl.multiple_of(c * 448 + 224, 32), 224)
    onward = [
        copy(WF.at[0], WX.at[2, lower], w_s.at[8], w_r.at[8], xdev(1)),
        copy(WF.at[1], WX.at[2, upper], w_s.at[9], w_r.at[9], xdev(-1)),
    ]
    both = [
        copy(WX.at[r, pl.ds(half, 448)], WX.at[r, pl.ds(half, 448)], w_s.at[9 + r], w_r.at[9 + r], {"dp": 1 - c})
        for r in (1, 2, 3)
    ]

    for s in range(1, 5):
        small_landed(s)
        if s < 4:
            small(s, s + 1, 1)
            small_landed(N - s)
            if s < 3:
                small(N - s, N - s - 1, -1)
        first_hop(s)
        if s < 4:
            first_hop(N - s)
    go(AUX.at[0], AUX.at[1], U2 + 1, zdev(1))
    go(AUX.at[0], AUX.at[7], U2 + 7, zdev(-1))

    for d in range(1, 4):
        for h in range(2):
            part = slice(4 * h, 4 * h + 4)
            for big, base, dev in ((XA, A2, zdev), (XB, B2, ydev)):
                landed(big.at[d, part], base + 2 * d + h)
                if d < 3 or h == 0:
                    go(big.at[d, part], big.at[d + 1, part], base + 2 * d + 2 + h, dev(1))
                landed(big.at[N - d, part], base + 2 * (N - d) + h)
                if d < 3 or h == 1:
                    go(big.at[N - d, part], big.at[N - d - 1, part], base + 2 * (N - d - 1) + h, dev(-1))
        landed(AUX.at[d], U2 + d)
        go(AUX.at[d], AUX.at[d + 1], U2 + d + 1, zdev(1))
        landed(AUX.at[N - d], U2 + N - d)
        if d < 3:
            go(AUX.at[N - d], AUX.at[N - d - 1], U2 + N - d - 1, zdev(-1))
        if d == 1:
            for w in far:
                w.wait_recv()
            for w in onward:
                w.start()
            for w in near:
                w.wait_recv()
            both[0].start()
            both[2].start()
        if d == 2:
            for w in onward:
                w.wait_recv()
            both[1].start()
    for h in range(2):
        part = slice(4 * h, 4 * h + 4)
        landed(XA.at[4, part], A2 + 8 + h)
        landed(XB.at[4, part], B2 + 8 + h)
    landed(AUX.at[4], U2 + 4)
    for d in local:
        d.wait()
    for d in both:
        d.wait_recv()

    mine = pl.ds(pl.multiple_of(t * 128, 128), 128)
    left_lanes = pl.ds(pl.multiple_of(((t + 3) % X) * 128, 128), 128)
    right_lanes = pl.ds(pl.multiple_of(((t + 1) % X) * 128, 128), 128)
    lo, hi = pl.ds(0, 64), pl.ds(64, 64)

    def xs(n, k):
        return x_s.at[n * 8 + k], x_r.at[n * 8 + k]

    def d_x1(n):
        return [
            copy(SX.at[n, 1, lo], T1.at[n, lo], *xs(n, 0), xdev(1)),
            copy(SX.at[n, 1, hi], T1.at[n, hi], *xs(n, 1), xdev(-1)),
        ]

    def d_x2(n):
        return [
            copy(SX.at[n, 0], R2.at[n, 0], *xs(n, 2), xdev(1)),
            copy(SX.at[n, 2], R2.at[n, 1], *xs(n, 3), xdev(-1)),
        ]

    def d_h(n):
        return [
            copy(HB.at[n, :, mine], HB.at[n, :, mine], *xs(n, 4), xdev(1)),
            copy(HB.at[n, :, mine], HB.at[n, :, mine], *xs(n, 5), xdev(-1)),
        ]

    def d_hf(n):
        return [
            copy(HB.at[n, lo, left_lanes], HB.at[n, lo, left_lanes], *xs(n, 6), xdev(1)),
            copy(HB.at[n, hi, right_lanes], HB.at[n, hi, right_lanes], *xs(n, 7), xdev(-1)),
        ]

    def d_b(n, h):
        a, b = n * 8 + 2 * h, n * 8 + 2 * h + 1
        if h == 0:
            lefts, rights = (CB.at[n, 4, :, 0:CUT], RB.at[n, 3, :, 0:CUT]), (CB.at[n, 4, :, CUT:896], RB.at[n, 5, :, CUT:896])
        else:
            lefts, rights = (CB.at[n, 4 - h], RB.at[n, 3 - h]), (CB.at[n, 4 + h], RB.at[n, 5 + h])
        return [
            copy(*lefts, b_s.at[a], b_r.at[a], ydev(-1)),
            copy(*rights, b_s.at[b], b_r.at[b], ydev(1)),
        ]

    def d_fb(j):
        return copy(SB.at[j], FB.at[j], fb_s.at[j], fb_r.at[j], zdev(-j))

    def d_fa(k):
        return copy(SA.at[k], FA.at[k], fa_s.at[k], fa_r.at[k], ydev(-k))

    def d_ra0():
        return [
            copy(CA.at[0, lo], RA.at[3, lo], ra_s.at[0], ra_r.at[3], zdev(-1)),
            copy(CA.at[0, hi], RA.at[5, hi], ra_s.at[7], ra_r.at[5], zdev(1)),
        ]

    def d_ra_left(n):
        j = 4 - (n + 1) // 2
        return copy(CA.at[n], RA.at[j - 1], ra_s.at[n], ra_r.at[j - 1], zdev(-1))

    def d_ra_right(n):
        j = 4 + n // 2
        return copy(CA.at[n], RA.at[j + 1], ra_s.at[n], ra_r.at[j + 1], zdev(1))

    def ra_landed(ref, slot):
        pltpu.make_async_copy(ref, ref, ra_r.at[slot]).wait()

    def start(ds):
        for d in ds:
            d.start()

    def arrived(ds):
        for d in ds:
            d.wait_recv()

    def dot(a, b):
        return jnp.dot(a, b, preferred_element_type=F32)

    def s0(n):
        j = group_of(n)
        lane8, sub8 = iota((8, 128), 1), iota((8, 128), 0)
        pick = (sub8 % 4 == e // 8) & (lane8 // HALF == e % 8)
        packed = jnp.zeros((8, 128), F32)
        for k in range(N):
            w = jnp.where(pick, AUX[j, k], 0.0)
            packed = packed + (w if k == 0 else pltpu.roll(w, k * HALF, 1))
        packed = pltpu.roll(packed, ((8 - e % 8) % 8) * HALF, 1)
        g_a = jnp.sum(jnp.where(sub8 < 4, packed, 0.0), axis=0, keepdims=True)
        g_b = jnp.sum(jnp.where(sub8 >= 4, packed, 0.0), axis=0, keepdims=True)
        m_a, m_b = g_a > 0.0, g_b > 0.0
        marks = jnp.concatenate(
            [
                jnp.broadcast_to(jnp.where(m_a, 1.0, 0.0), (8, 128)),
                jnp.broadcast_to(jnp.where(m_b, 1.0, 0.0), (8, 128)),
            ],
            axis=0,
        ).astype(BF)
        r_i, l_i = iota((128, 128), 0), iota((128, 128), 1)
        same = r_i // HALF == l_i // HALF
        before = dot(marks, jnp.where(same & (r_i < l_i), 1.0, 0.0).astype(BF))
        whole = dot(marks, jnp.where(same, 1.0, 0.0).astype(BF))
        base = ((iota((1, 128), 1) // HALF) * HALF).astype(F32)
        code_a = jnp.where(m_a, base + before[0:1], -1.0)
        code_b = jnp.where(m_b, base + before[8:9] + whole[0:1], -1.0)
        row = r_i.astype(F32)
        p_a = jnp.where(code_a == row, 1.0, 0.0)
        p_b = jnp.where(code_b == row, 1.0, 0.0)
        GS[n] = jnp.sum(p_a * g_a + p_b * g_b, axis=1, keepdims=True)
        PT[n, 0:128] = p_a.T.astype(BF)
        PT[n, 128:256] = p_b.T.astype(BF)
        place = jnp.concatenate([p_a, p_b], axis=1).astype(BF)
        rows = jnp.concatenate([XA[j].reshape(128, 896), XB[:, j].reshape(128, 896)], axis=0)
        routed = dot(place, rows).astype(BF)
        SX[n, 1] = dot(routed, WX[2]).astype(BF)
        start(d_x1(n))
        to_right = dot(routed, WX[1])
        NB[n, 0] = to_right[0:64]
        SX[n, 0, 64:128] = to_right[64:128].astype(BF)
        to_left = dot(routed, WX[3])
        NB[n, 1] = to_left[64:128]
        SX[n, 2, 0:64] = to_left[0:64].astype(BF)
        OWN[n] = dot(routed, WX[0])

    def s1(n):
        arrived(d_x1(n))
        SX[n, 0, 0:64] = (NB[n, 0] + T1[n, 0:64].astype(F32)).astype(BF)
        SX[n, 2, 64:128] = (NB[n, 1] + T1[n, 64:128].astype(F32)).astype(BF)
        start(d_x2(n))

    def s2(n):
        arrived(d_x2(n))
        pre = OWN[n] + R2[n, 0].astype(F32) + R2[n, 1].astype(F32)
        gate, up = pre[:, 0:128], pre[:, 128:256]
        HB[n, :, mine] = (gate * jax.nn.sigmoid(gate) * up).astype(BF)
        start(d_h(n))

    def s3(n):
        arrived(d_h(n))
        start(d_hf(n))

    def s4(n):
        arrived(d_hf(n))
        result = (dot(HB[n], WD[...]) * GS[n]).astype(BF)
        back = dot(PT[n], result).astype(BF)
        CA[n] = back[0:128]
        CB[n] = back[128:256].reshape(8, HALF, 896)
        start(d_b(n, 0))

        @pl.when(n == 0)
        def _():
            start(d_ra0())

        @pl.when(n == 1)
        def _():
            ra_landed(RA.at[3, lo], 3)
            CA[1, 0:64] = CA[1, 0:64] + RA[3, 0:64]
            d_ra_left(1).start()

        @pl.when(n == 2)
        def _():
            ra_landed(RA.at[5, hi], 5)
            CA[2, 64:128] = CA[2, 64:128] + RA[5, 64:128]
            d_ra_right(2).start()

        @pl.when((n == 3) | (n == 5))
        def _():
            j = 4 - (n + 1) // 2
            ra_landed(RA.at[j], j)
            CA[n] = CA[n] + RA[j]
            d_ra_left(n).start()

        @pl.when((n == 4) | (n == 6))
        def _():
            j = 4 + n // 2
            ra_landed(RA.at[j], j)
            CA[n] = CA[n] + RA[j]
            d_ra_right(n).start()

        @pl.when(n == 7)
        def _():
            ra_landed(RA.at[0], 0)
            ra_landed(RA.at[8], 8)
            for k in range(7, -1, -1):
                piece = pl.ds(k * HALF, HALF)
                total = CA[7, piece].astype(F32) + RA[0, piece].astype(F32) + RA[8, piece].astype(F32)
                if k == 0:
                    TA[...] = total
                else:
                    SA[k] = total.astype(BF)
                    d_fa(k).start()

    def s5(n, h):
        arrived(d_b(n, h - 1))
        if h == 1:
            CB[n, 3, :, 0:CUT] = CB[n, 3, :, 0:CUT] + RB[n, 3, :, 0:CUT]
            CB[n, 5, :, CUT:896] = CB[n, 5, :, CUT:896] + RB[n, 5, :, CUT:896]
        else:
            CB[n, 4 - h] = CB[n, 4 - h] + RB[n, 4 - h]
            CB[n, 4 + h] = CB[n, 4 + h] + RB[n, 4 + h]
        start(d_b(n, h))

    def s8(n):
        arrived(d_b(n, 3))
        j = group_of(n)
        total = CB[n, 0].astype(F32) + RB[n, 0].astype(F32) + RB[n, 8].astype(F32)

        @pl.when(n < 7)
        def _():
            SB[j] = total.astype(BF)
            d_fb(j).start()

        @pl.when(n == 7)
        def _():
            TB[...] = total

    stages = [
        (3, s3),
        (2, s2),
        (1, s1),
        (0, s0),
        (8, s8),
        (7, functools.partial(s5, h=3)),
        (6, functools.partial(s5, h=2)),
        (5, functools.partial(s5, h=1)),
        (4, s4),
    ]

    def turn(i, carry):
        for lag, stage in stages:

            @pl.when((i >= lag) & (i < lag + GROUPS))
            def _():
                stage(i - lag)

        return carry

    lax.fori_loop(0, GROUPS + 8, turn, 0)

    total_a, total_b = TA[...], TB[...]
    for k in range(1, N):
        d_fa(k).wait_recv()
        total_a = total_a + FA[k].astype(F32)
    for k in range(1, N):
        d_fb(k).wait_recv()
        total_b = total_b + FB[k].astype(F32)
    out[0:HALF] = total_a.astype(BF)
    out[HALF : 2 * HALF] = total_b.astype(BF)

    for d in sent + near + far + onward + both + d_ra0():
        d.wait_send()
    for n in (1, 3, 5):
        d_ra_left(n).wait_send()
    for n in (2, 4, 6):
        d_ra_right(n).wait_send()

    def drain(n, carry):
        for d in d_x1(n) + d_x2(n) + d_h(n) + d_hf(n):
            d.wait_send()
        for h in range(4):
            for d in d_b(n, h):
                d.wait_send()
        return carry

    lax.fori_loop(0, GROUPS, drain, 0)

    def drain_small(k, carry):
        d_fa(k).wait_send()
        d_fb(k).wait_send()
        return carry

    lax.fori_loop(1, N, drain_small, 0)


def on_device(tokens, dither, expert_ids, gate_values, gate_weight, up_weight, down_weight):
    rows, quarter = tokens.shape
    vmem = pl.BlockSpec(memory_space=pltpu.VMEM)
    hbm = pl.BlockSpec(memory_space=pl.ANY)
    dma = pltpu.SemaphoreType.DMA
    return pl.pallas_call(
        kernel,
        out_shape=jax.ShapeDtypeStruct((rows, quarter), BF),
        in_specs=[vmem] * 4 + [hbm] * 3,
        out_specs=vmem,
        scratch_shapes=[
            pltpu.VMEM((8, 8, HALF, 896), BF),
            pltpu.VMEM((8, 8, HALF, 896), BF),
            pltpu.VMEM((8, 8, 8, 128), F32),
            pltpu.VMEM((4, 896, 256), BF),
            pltpu.VMEM((2, 224, 256), BF),
            pltpu.VMEM((512, 896), BF),
            pltpu.VMEM((8, 256, 128), BF),
            pltpu.VMEM((8, 128, 1), F32),
            pltpu.VMEM((8, 128, 256), F32),
            pltpu.VMEM((8, 2, 64, 256), F32),
            pltpu.VMEM((8, 3, 128, 256), BF),
            pltpu.VMEM((8, 128, 256), BF),
            pltpu.VMEM((8, 2, 128, 256), BF),
            pltpu.VMEM((8, 128, 512), BF),
            pltpu.VMEM((8, 128, 896), BF),
            pltpu.VMEM((9, 128, 896), BF),
            pltpu.VMEM((8, 8, HALF, 896), BF),
            pltpu.VMEM((8, 9, HALF, 896), BF),
            pltpu.VMEM((8, HALF, 896), BF),
            pltpu.VMEM((8, HALF, 896), BF),
            pltpu.VMEM((8, HALF, 896), BF),
            pltpu.VMEM((8, HALF, 896), BF),
            pltpu.VMEM((HALF, 896), F32),
            pltpu.VMEM((HALF, 896), F32),
            dma((96,)),
            dma((64,)),
            dma((13,)),
            dma((13,)),
            dma((3,)),
            dma((64,)),
            dma((64,)),
            dma((8,)),
            dma((9,)),
            dma((64,)),
            dma((64,)),
            dma((8,)),
            dma((8,)),
            dma((8,)),
            dma((8,)),
        ],
        compiler_params=pltpu.CompilerParams(
            collective_id=0, has_side_effects=True, vmem_limit_bytes=48 * 1024 * 1024
        ),
        cost_estimate=pl.CostEstimate(flops=5_000_000_000, bytes_accessed=4_000_000, transcendentals=200_000),
    )(tokens, dither.reshape(1, rows), expert_ids, gate_values, gate_weight, up_weight, down_weight)


def solution(mesh):
    in_specs = (
        P(("dp", "expert"), "tensor"),
        P(("dp", "expert")),
        P(("dp", "expert"), None),
        P(("dp", "expert"), None),
        P("expert", None, "tensor"),
        P("expert", None, "tensor"),
        P("expert", None, "tensor"),
    )
    return jax.shard_map(
        on_device, mesh=mesh, in_specs=in_specs, out_specs=P(("dp", "expert"), "tensor"), check_vma=False
    )
```

```python
import functools

import jax
import jax.numpy as jnp
from jax import lax
from jax.experimental import pallas as pl
from jax.experimental.pallas import tpu as pltpu
from jax.sharding import PartitionSpec as P

MESH = pl.DeviceIdType.MESH
BF = jnp.bfloat16
F32 = jnp.float32
N = 8
X = 4
HALF = 16
GROUPS = 8
CUT = 512
NEAREST = (1, 7, 2, 6, 3, 5, 4)
STAGGER = False
LAG = 2
HOP = 2


def iota(shape, axis):
    return lax.broadcasted_iota(jnp.int32, shape, axis)


def dither_round(values, dither_row, column_start):
    rows, cols = values.shape
    scaled = values.astype(F32)
    magnitude = jnp.abs(scaled)
    grid = jnp.full_like(scaled, 2.0**-26)
    inverse = jnp.full_like(scaled, 2.0**26)
    for octave in range(-23, 4):
        above = magnitude >= 2.0**octave
        grid = jnp.where(above, 2.0 ** (octave - 2), grid)
        inverse = jnp.where(above, 2.0 ** (2 - octave), inverse)
    square = jnp.broadcast_to(dither_row.astype(F32), (rows, rows))
    diagonal = iota((rows, rows), 0) == iota((rows, rows), 1)
    column = jnp.sum(jnp.where(diagonal, square, 0.0), axis=1, keepdims=True).astype(jnp.int32)
    offset = (column + 97 * (column_start + iota((rows, cols), 1))) & 255
    jitter = (offset.astype(F32) + 0.5) / 256.0
    return (jnp.floor(scaled * inverse + jitter) * grid).astype(BF)


def gate_table(ids, gates):
    rows = []
    expert = iota((8, 128), 1) // HALF
    for h in range(2):
        part = slice(h * HALF, h * HALF + HALF)
        wide_ids = jnp.concatenate([ids[:, part]] * 8, axis=1)
        wide_gates = jnp.concatenate([gates[:, part]] * 8, axis=1)
        for r in range(4):
            chosen = jnp.where(wide_ids == expert + 8 * r, wide_gates, 0.0)
            rows.append(jnp.sum(chosen, axis=0, keepdims=True))
    return jnp.concatenate(rows, axis=0)


def group_of(n):
    return jnp.where(n % 2 == 1, 4 - (n + 1) // 2, 4 + n // 2)


def kernel(
    tok_h, dit, ids, gat, gw, uw, dw, out,
    TOK, PP, XA, XB, AUX, WX, WF, WD, PT, GS, OWN, NB, SX, T1, R2, HB, CA, RA, CB, RB, FA, FB, SA, SB, TA, TB,
    ag_s, ag_r, w_s, w_r, w_l, x_s, x_r, ra_s, ra_r, b_s, b_r, fa_s, fa_r, fb_s, fb_r, turn_sem,
):
    here = lax.axis_index("expert")
    t = lax.axis_index("tensor")
    c = lax.axis_index("dp")
    y, z = here % N, here // N
    e = here // 2

    def ydev(k):
        return {"expert": z * N + (y + k + N) % N}

    def zdev(k):
        return {"expert": ((z + k + N) % N) * N + y}

    def xdev(k):
        return {"tensor": (t + k + X) % X}

    def copy(src, dst, ss, rs, dev):
        return pltpu.make_async_remote_copy(
            src_ref=src, dst_ref=dst, send_sem=ss, recv_sem=rs, device_id=dev, device_id_type=MESH
        )

    barrier = pltpu.get_barrier_semaphore()
    peers = [ydev(k) for k in range(1, N)] + [zdev(k) for k in range(1, N)]
    peers += [xdev(1), xdev(-1), {"dp": 1 - c}]
    for peer in peers:
        pl.semaphore_signal(barrier, inc=1, device_id=peer, device_id_type=MESH)

    local = [
        pltpu.make_async_copy(dw.at[0], WD, w_l.at[0]),
        pltpu.make_async_copy(gw.at[0, pl.ds(pl.multiple_of(t * 896, 128), 896)], WX.at[0, :, 0:128], w_l.at[1]),
        pltpu.make_async_copy(uw.at[0, pl.ds(pl.multiple_of(t * 896, 128), 896)], WX.at[0, :, 128:256], w_l.at[2]),
    ]
    first = pltpu.make_async_copy(tok_h, TOK, w_l.at[3])
    first.start()
    for d in local:
        d.start()
    AUX[0, 0] = gate_table(ids[...], gat[...])
    first.wait()
    block = dither_round(TOK[...], dit[...], t * TOK.shape[1])
    XA[0, 0] = block[:HALF]
    XB[0, 0] = block[HALF:]
    pl.semaphore_wait(barrier, len(peers))

    def dot(a, b):
        return jnp.dot(a, b, preferred_element_type=F32)

    def prepare(j):
        lane8, sub8 = iota((8, 128), 1), iota((8, 128), 0)
        pick = (sub8 % 4 == e // 8) & (lane8 // HALF == e % 8)
        packed = jnp.zeros((8, 128), F32)
        for k in range(N):
            w = jnp.where(pick, AUX[j, k], 0.0)
            packed = packed + (w if k == 0 else pltpu.roll(w, k * HALF, 1))
        packed = pltpu.roll(packed, ((8 - e % 8) % 8) * HALF, 1)
        g_a = jnp.sum(jnp.where(sub8 < 4, packed, 0.0), axis=0, keepdims=True)
        g_b = jnp.sum(jnp.where(sub8 >= 4, packed, 0.0), axis=0, keepdims=True)
        m_a, m_b = g_a > 0.0, g_b > 0.0
        marks = jnp.concatenate(
            [
                jnp.broadcast_to(jnp.where(m_a, 1.0, 0.0), (8, 128)),
                jnp.broadcast_to(jnp.where(m_b, 1.0, 0.0), (8, 128)),
            ],
            axis=0,
        ).astype(BF)
        r_i, l_i = iota((128, 128), 0), iota((128, 128), 1)
        same = r_i // HALF == l_i // HALF
        before = dot(marks, jnp.where(same & (r_i < l_i), 1.0, 0.0).astype(BF))
        whole = dot(marks, jnp.where(same, 1.0, 0.0).astype(BF))
        base = ((iota((1, 128), 1) // HALF) * HALF).astype(F32)
        code_a = jnp.where(m_a, base + before[0:1], -1.0)
        code_b = jnp.where(m_b, base + before[8:9] + whole[0:1], -1.0)
        row = r_i.astype(F32)
        p_a = jnp.where(code_a == row, 1.0, 0.0)
        p_b = jnp.where(code_b == row, 1.0, 0.0)
        GS[j] = jnp.sum(p_a * g_a + p_b * g_b, axis=1, keepdims=True)
        PT[j, 0:128] = p_a.T.astype(BF)
        PT[j, 128:256] = p_b.T.astype(BF)
        PP[j] = jnp.concatenate([p_a, p_b], axis=1).astype(BF)
    sent = []
    counter = [0]

    def go(src, dst, rs, dev):
        d = copy(src, dst, ag_s.at[counter[0]], ag_r.at[rs], dev)
        counter[0] += 1
        d.start()
        sent.append(d)

    def landed(ref, rs):
        pltpu.make_async_copy(ref, ref, ag_r.at[rs]).wait()

    A1, U1, B1 = 0, 8, 16
    A2, B2, U2 = 24, 40, 56

    def first_hop(k):
        h = k // 4
        go(XA.at[0, k], XA.at[1, k], A2 + 2 + h, zdev(1))
        go(XA.at[0, k], XA.at[7, k], A2 + 14 + h, zdev(-1))
        go(XB.at[0, k], XB.at[1, k], B2 + 2 + h, ydev(1))
        go(XB.at[0, k], XB.at[7, k], B2 + 14 + h, ydev(-1))

    def small_landed(k):
        landed(XA.at[0, k], A1 + k)
        landed(AUX.at[0, k], U1 + k)
        landed(XB.at[0, k], B1 + k)

    for k in NEAREST:
        go(XA.at[0, 0], XA.at[0, k], A1 + k, ydev(k))
        go(AUX.at[0, 0], AUX.at[0, k], U1 + k, ydev(k))
        go(XB.at[0, 0], XB.at[0, k], B1 + k, zdev(k))

    half = pl.multiple_of(c * 448, 64)
    wide = (slice(0, 128), slice(128, 256))

    def rows_for(k, start, size):
        return pl.ds(pl.multiple_of(((t + k + X) % X) * 896 + c * 448 + start, 32), size)

    near, far = [], []
    for p, w in enumerate((gw, uw)):
        near.append(copy(w.at[0, rows_for(1, 0, 448)], WX.at[3, pl.ds(half, 448), wide[p]], w_s.at[p], w_r.at[p], xdev(1)))
        near.append(copy(w.at[0, rows_for(-1, 0, 448)], WX.at[1, pl.ds(half, 448), wide[p]], w_s.at[2 + p], w_r.at[2 + p], xdev(-1)))
        far.append(copy(w.at[0, rows_for(2, 0, 224)], WF.at[0, :, wide[p]], w_s.at[4 + p], w_r.at[4 + p], xdev(1)))
        far.append(copy(w.at[0, rows_for(2, 224, 224)], WF.at[1, :, wide[p]], w_s.at[6 + p], w_r.at[6 + p], xdev(-1)))
    for d in far + near:
        d.start()
    lower = pl.ds(pl.multiple_of(c * 448, 32), 224)
    upper = pl.ds(pl.multiple_of(c * 448 + 224, 32), 224)
    onward = [
        copy(WF.at[0], WX.at[2, lower], w_s.at[8], w_r.at[8], xdev(1)),
        copy(WF.at[1], WX.at[2, upper], w_s.at[9], w_r.at[9], xdev(-1)),
    ]
    both = [
        copy(WX.at[r, pl.ds(half, 448)], WX.at[r, pl.ds(half, 448)], w_s.at[9 + r], w_r.at[9 + r], {"dp": 1 - c})
        for r in (1, 2, 3)
    ]

    def recut():
        for w in far:
            w.wait_recv()
        for w in onward:
            w.start()
        for w in near:
            w.wait_recv()
        both[0].start()
        both[2].start()

    def recut_end():
        for w in onward:
            w.wait_recv()
        both[1].start()

    if STAGGER:

        @pl.when(c == 1)
        def _():
            recut()
            recut_end()
            pl.semaphore_wait(turn_sem, 1)

    first_hop(0)
    for k in NEAREST:
        small_landed(k)
        first_hop(k)
    go(AUX.at[0], AUX.at[1], U2 + 1, zdev(1))
    go(AUX.at[0], AUX.at[7], U2 + 7, zdev(-1))

    for d in range(1, 4):
        for h in range(2):
            part = slice(4 * h, 4 * h + 4)
            for big, base, dev in ((XA, A2, zdev), (XB, B2, ydev)):
                landed(big.at[d, part], base + 2 * d + h)
                if d < 3 or h == 0:
                    go(big.at[d, part], big.at[d + 1, part], base + 2 * d + 2 + h, dev(1))
                landed(big.at[N - d, part], base + 2 * (N - d) + h)
                if d < 3 or h == 1:
                    go(big.at[N - d, part], big.at[N - d - 1, part], base + 2 * (N - d - 1) + h, dev(-1))
        landed(AUX.at[d], U2 + d)
        go(AUX.at[d], AUX.at[d + 1], U2 + d + 1, zdev(1))
        landed(AUX.at[N - d], U2 + N - d)
        if d < 3:
            go(AUX.at[N - d], AUX.at[N - d - 1], U2 + N - d - 1, zdev(-1))
        if d == 1:
            if STAGGER:
                pl.when(c == 0)(recut)
            else:
                recut()
            prepare(0)
        if d == 2:
            if STAGGER:
                pl.when(c == 0)(recut_end)
            else:
                recut_end()
        prepare(d)
        prepare(N - d)
    if STAGGER:

        @pl.when(c == 0)
        def _():
            pl.semaphore_signal(turn_sem, inc=1, device_id={"dp": 1 - c}, device_id_type=MESH)

    for h in range(2):
        part = slice(4 * h, 4 * h + 4)
        landed(XA.at[4, part], A2 + 8 + h)
        landed(XB.at[4, part], B2 + 8 + h)
    landed(AUX.at[4], U2 + 4)
    prepare(4)
    for d in local:
        d.wait()
    for d in both:
        d.wait_recv()

    mine = pl.ds(pl.multiple_of(t * 128, 128), 128)
    left_lanes = pl.ds(pl.multiple_of(((t + 3) % X) * 128, 128), 128)
    right_lanes = pl.ds(pl.multiple_of(((t + 1) % X) * 128, 128), 128)
    lo, hi = pl.ds(0, 64), pl.ds(64, 64)

    def xs(n, k):
        return x_s.at[n * 8 + k], x_r.at[n * 8 + k]

    def d_x1(n):
        return [
            copy(SX.at[n, 1, lo], T1.at[n, lo], *xs(n, 0), xdev(1)),
            copy(SX.at[n, 1, hi], T1.at[n, hi], *xs(n, 1), xdev(-1)),
        ]

    def d_x2(n):
        return [
            copy(SX.at[n, 0], R2.at[n, 0], *xs(n, 2), xdev(1)),
            copy(SX.at[n, 2], R2.at[n, 1], *xs(n, 3), xdev(-1)),
        ]

    def d_h(n):
        return [
            copy(HB.at[n, :, mine], HB.at[n, :, mine], *xs(n, 4), xdev(1)),
            copy(HB.at[n, :, mine], HB.at[n, :, mine], *xs(n, 5), xdev(-1)),
        ]

    def d_hf(n):
        return [
            copy(HB.at[n, lo, left_lanes], HB.at[n, lo, left_lanes], *xs(n, 6), xdev(1)),
            copy(HB.at[n, hi, right_lanes], HB.at[n, hi, right_lanes], *xs(n, 7), xdev(-1)),
        ]

    def d_b(n, h):
        a, b = n * 8 + 2 * h, n * 8 + 2 * h + 1
        if h == 0:
            lefts, rights = (CB.at[n, 4, :, 0:CUT], RB.at[n, 3, :, 0:CUT]), (CB.at[n, 4, :, CUT:896], RB.at[n, 5, :, CUT:896])
        else:
            lefts, rights = (CB.at[n, 4 - h], RB.at[n, 3 - h]), (CB.at[n, 4 + h], RB.at[n, 5 + h])
        return [
            copy(*lefts, b_s.at[a], b_r.at[a], ydev(-1)),
            copy(*rights, b_s.at[b], b_r.at[b], ydev(1)),
        ]

    def d_fb(j):
        return copy(SB.at[j], FB.at[j], fb_s.at[j], fb_r.at[j], zdev(-j))

    def d_fa(k):
        return copy(SA.at[k], FA.at[k], fa_s.at[k], fa_r.at[k], ydev(-k))

    def d_ra0():
        return [
            copy(CA.at[0, lo], RA.at[3, lo], ra_s.at[0], ra_r.at[6], zdev(-1)),
            copy(CA.at[0, hi], RA.at[5, hi], ra_s.at[1], ra_r.at[11], zdev(1)),
        ]

    def d_ra_left(n, h):
        j = 4 - (n + 1) // 2
        part = (lo, hi)[h]
        return copy(CA.at[n, part], RA.at[j - 1, part], ra_s.at[2 * n + h], ra_r.at[2 * j - 2 + h], zdev(-1))

    def d_ra_right(n, h):
        j = 4 + n // 2
        part = (lo, hi)[h]
        return copy(CA.at[n, part], RA.at[j + 1, part], ra_s.at[2 * n + h], ra_r.at[2 * j + 2 + h], zdev(1))

    def ra_landed(ref, slot):
        pltpu.make_async_copy(ref, ref, ra_r.at[slot]).wait()

    def start(ds):
        for d in ds:
            d.start()

    def arrived(ds):
        for d in ds:
            d.wait_recv()

    def s0(n):
        j = group_of(n)
        rows = jnp.concatenate([XA[j].reshape(128, 896), XB[:, j].reshape(128, 896)], axis=0)
        routed = dot(PP[j], rows).astype(BF)
        SX[n, 1] = dot(routed, WX[2]).astype(BF)
        start(d_x1(n))
        to_right = dot(routed, WX[1])
        NB[n, 0] = to_right[0:64]
        SX[n, 0, 64:128] = to_right[64:128].astype(BF)
        to_left = dot(routed, WX[3])
        NB[n, 1] = to_left[64:128]
        SX[n, 2, 0:64] = to_left[0:64].astype(BF)
        OWN[n] = dot(routed, WX[0])

    def s1(n):
        arrived(d_x1(n))
        SX[n, 0, 0:64] = (NB[n, 0] + T1[n, 0:64].astype(F32)).astype(BF)
        SX[n, 2, 64:128] = (NB[n, 1] + T1[n, 64:128].astype(F32)).astype(BF)
        start(d_x2(n))

    def s2(n):
        arrived(d_x2(n))
        pre = OWN[n] + R2[n, 0].astype(F32) + R2[n, 1].astype(F32)
        gate, up = pre[:, 0:128], pre[:, 128:256]
        HB[n, :, mine] = (gate * jax.nn.sigmoid(gate) * up).astype(BF)
        start(d_h(n))

    def s3(n):
        arrived(d_h(n))
        start(d_hf(n))

    def s4(n):
        arrived(d_hf(n))
        j = group_of(n)
        result = (dot(HB[n], WD[...]) * GS[j]).astype(BF)
        back = dot(PT[j], result).astype(BF)
        CA[n] = back[0:128]
        CB[n] = back[128:256].reshape(8, HALF, 896)

        start(d_b(n, 0))

        @pl.when(n == 0)
        def _():
            start(d_ra0())

        @pl.when(n % 2 == 1)
        def _():
            j = 4 - (n + 1) // 2

            @pl.when(n < 7)
            def _():
                for h, part in enumerate((lo, hi)):
                    if h == 0:
                        ra_landed(RA.at[j, part], 2 * j + h)
                        CA[n, part] = CA[n, part] + RA[j, part]
                    else:

                        @pl.when(n > 1)
                        def _():
                            ra_landed(RA.at[j, part], 2 * j + h)
                            CA[n, part] = CA[n, part] + RA[j, part]

                    d_ra_left(n, h).start()

        @pl.when((n % 2 == 0) & (n > 0))
        def _():
            j = 4 + n // 2
            for h, part in ((1, hi), (0, lo)):
                if h == 1:
                    ra_landed(RA.at[j, part], 2 * j + h)
                    CA[n, part] = CA[n, part] + RA[j, part]
                else:

                    @pl.when(n > 2)
                    def _():
                        ra_landed(RA.at[j, part], 2 * j + h)
                        CA[n, part] = CA[n, part] + RA[j, part]

                d_ra_right(n, h).start()

        @pl.when(n == 7)
        def _():
            for h, part in enumerate((lo, hi)):
                ra_landed(RA.at[0, part], h)
                ra_landed(RA.at[8, part], 16 + h)
            for k in range(7, -1, -1):
                piece = pl.ds(k * HALF, HALF)
                total = CA[7, piece].astype(F32) + RA[0, piece].astype(F32) + RA[8, piece].astype(F32)
                if k == 0:
                    TA[...] = total
                else:
                    SA[k] = total.astype(BF)
                    d_fa(k).start()

    def s5(n, h):
        arrived(d_b(n, h - 1))
        if h == 1:
            CB[n, 3, :, 0:CUT] = CB[n, 3, :, 0:CUT] + RB[n, 3, :, 0:CUT]
            CB[n, 5, :, CUT:896] = CB[n, 5, :, CUT:896] + RB[n, 5, :, CUT:896]
        else:
            CB[n, 4 - h] = CB[n, 4 - h] + RB[n, 4 - h]
            CB[n, 4 + h] = CB[n, 4 + h] + RB[n, 4 + h]
        start(d_b(n, h))

    def s8(n):
        arrived(d_b(n, 3))
        j = group_of(n)
        total = CB[n, 0].astype(F32) + RB[n, 0].astype(F32) + RB[n, 8].astype(F32)

        @pl.when(n < 7)
        def _():
            SB[j] = total.astype(BF)
            d_fb(j).start()

        @pl.when(n == 7)
        def _():
            TB[...] = total

    last = 4 * LAG
    stages = [
        (1 * LAG, 0, 8, s1),
        (2 * LAG, 0, 8, s2),
        (3 * LAG, 0, 8, s3),
        (0, 0, 8, s0),
        (last, 0, 8, s4),
        (last + 4 * HOP, 0, 8, s8),
        (last + 3 * HOP, 0, 8, functools.partial(s5, h=3)),
        (last + 2 * HOP, 0, 8, functools.partial(s5, h=2)),
        (last + 1 * HOP, 0, 8, functools.partial(s5, h=1)),
    ]
    turns = max(lag + to for lag, _, to, _ in stages)

    def turn(i, carry):
        for lag, since, to, stage in stages:

            @pl.when((i >= lag + since) & (i < lag + to))
            def _():
                stage(i - lag)

        return carry

    lax.fori_loop(0, turns, turn, 0)

    total_a, total_b = TA[...], TB[...]
    for k in range(1, N):
        d_fa(k).wait_recv()
        total_a = total_a + FA[k].astype(F32)
    for k in range(1, N):
        d_fb(k).wait_recv()
        total_b = total_b + FB[k].astype(F32)
    out[0:HALF] = total_a.astype(BF)
    out[HALF : 2 * HALF] = total_b.astype(BF)

    for d in sent + near + far + onward + both + d_ra0():
        d.wait_send()
    for h in range(2):
        for n in (1, 3, 5):
            d_ra_left(n, h).wait_send()
        for n in (2, 4, 6):
            d_ra_right(n, h).wait_send()

    def drain(n, carry):
        for d in d_x1(n) + d_x2(n) + d_h(n) + d_hf(n):
            d.wait_send()

        for h in range(4):
            for d in d_b(n, h):
                d.wait_send()
        return carry

    lax.fori_loop(0, GROUPS, drain, 0)

    def drain_small(k, carry):
        d_fa(k).wait_send()
        d_fb(k).wait_send()
        return carry

    lax.fori_loop(1, N, drain_small, 0)


def on_device(tokens, dither, expert_ids, gate_values, gate_weight, up_weight, down_weight):
    rows, quarter = tokens.shape
    vmem = pl.BlockSpec(memory_space=pltpu.VMEM)
    hbm = pl.BlockSpec(memory_space=pl.ANY)
    dma = pltpu.SemaphoreType.DMA
    return pl.pallas_call(
        kernel,
        out_shape=jax.ShapeDtypeStruct((rows, quarter), BF),
        in_specs=[hbm] + [vmem] * 3 + [hbm] * 3,
        out_specs=vmem,
        scratch_shapes=[
            pltpu.VMEM((rows, quarter), BF),
            pltpu.VMEM((8, 128, 256), BF),
            pltpu.VMEM((8, 8, HALF, 896), BF),
            pltpu.VMEM((8, 8, HALF, 896), BF),
            pltpu.VMEM((8, 8, 8, 128), F32),
            pltpu.VMEM((4, 896, 256), BF),
            pltpu.VMEM((2, 224, 256), BF),
            pltpu.VMEM((512, 896), BF),
            pltpu.VMEM((8, 256, 128), BF),
            pltpu.VMEM((8, 128, 1), F32),
            pltpu.VMEM((8, 128, 256), F32),
            pltpu.VMEM((8, 2, 64, 256), F32),
            pltpu.VMEM((8, 3, 128, 256), BF),
            pltpu.VMEM((8, 128, 256), BF),
            pltpu.VMEM((8, 2, 128, 256), BF),
            pltpu.VMEM((8, 128, 512), BF),
            pltpu.VMEM((8, 128, 896), BF),
            pltpu.VMEM((9, 128, 896), BF),
            pltpu.VMEM((8, 8, HALF, 896), BF),
            pltpu.VMEM((8, 9, HALF, 896), BF),
            pltpu.VMEM((8, HALF, 896), BF),
            pltpu.VMEM((8, HALF, 896), BF),
            pltpu.VMEM((8, HALF, 896), BF),
            pltpu.VMEM((8, HALF, 896), BF),
            pltpu.VMEM((HALF, 896), F32),
            pltpu.VMEM((HALF, 896), F32),
            dma((96,)),
            dma((64,)),
            dma((13,)),
            dma((13,)),
            dma((4,)),
            dma((64,)),
            dma((64,)),
            dma((16,)),
            dma((18,)),
            dma((64,)),
            dma((64,)),
            dma((8,)),
            dma((8,)),
            dma((8,)),
            dma((8,)),
            pltpu.SemaphoreType.REGULAR,
        ],
        compiler_params=pltpu.CompilerParams(
            collective_id=0, has_side_effects=True, vmem_limit_bytes=60 * 1024 * 1024
        ),
        cost_estimate=pl.CostEstimate(flops=5_000_000_000, bytes_accessed=4_000_000, transcendentals=200_000),
    )(tokens, dither.reshape(1, rows), expert_ids.T, gate_values.T, gate_weight, up_weight, down_weight)


def solution(mesh):
    in_specs = (
        P(("dp", "expert"), "tensor"),
        P(("dp", "expert")),
        P(("dp", "expert"), None),
        P(("dp", "expert"), None),
        P("expert", None, "tensor"),
        P("expert", None, "tensor"),
        P("expert", None, "tensor"),
    )
    return jax.shard_map(
        on_device, mesh=mesh, in_specs=in_specs, out_specs=P(("dp", "expert"), "tensor"), check_vma=False
    )
```

```python
import functools

import jax
import jax.numpy as jnp
from jax import lax
from jax.experimental import pallas as pl
from jax.experimental.pallas import tpu as pltpu
from jax.sharding import PartitionSpec as P

MESH = pl.DeviceIdType.MESH
BF = jnp.bfloat16
F32 = jnp.float32
N = 8
X = 4
HALF = 16
GROUPS = 8
CUT = 512
NEAREST = (1, 7, 2, 6, 3, 5, 4)
STAGGER = False
LAG = 2
HOP = 2


def iota(shape, axis):
    return lax.broadcasted_iota(jnp.int32, shape, axis)


def dither_round(values, dither_row, column_start):
    rows, cols = values.shape
    scaled = values.astype(F32)
    magnitude = jnp.abs(scaled)
    grid = jnp.full_like(scaled, 2.0**-26)
    inverse = jnp.full_like(scaled, 2.0**26)
    for octave in range(-23, 4):
        above = magnitude >= 2.0**octave
        grid = jnp.where(above, 2.0 ** (octave - 2), grid)
        inverse = jnp.where(above, 2.0 ** (2 - octave), inverse)
    square = jnp.broadcast_to(dither_row.astype(F32), (rows, rows))
    diagonal = iota((rows, rows), 0) == iota((rows, rows), 1)
    column = jnp.sum(jnp.where(diagonal, square, 0.0), axis=1, keepdims=True).astype(jnp.int32)
    offset = (column + 97 * (column_start + iota((rows, cols), 1))) & 255
    jitter = (offset.astype(F32) + 0.5) / 256.0
    return (jnp.floor(scaled * inverse + jitter) * grid).astype(BF)


def gate_table(ids, gates):
    rows = []
    expert = iota((8, 128), 1) // HALF
    for h in range(2):
        part = slice(h * HALF, h * HALF + HALF)
        wide_ids = jnp.concatenate([ids[:, part]] * 8, axis=1)
        wide_gates = jnp.concatenate([gates[:, part]] * 8, axis=1)
        for r in range(4):
            chosen = jnp.where(wide_ids == expert + 8 * r, wide_gates, 0.0)
            rows.append(jnp.sum(chosen, axis=0, keepdims=True))
    return jnp.concatenate(rows, axis=0)


def group_of(n):
    return jnp.where(n % 2 == 1, 4 - (n + 1) // 2, 4 + n // 2)


def kernel(
    tok_h, dit, ids, gat, gw, uw, dw, out,
    TOK, PP, XA, XB, AUX, WX, WF, WD, PT, GS, OWN, SX, R2, HB, CA, RA, CB, RB, FA, FB, SA, SB, TA, TB,
    ag_s, ag_r, w_s, w_r, w_l, x_s, x_r, ra_s, ra_r, b_s, b_r, fa_s, fa_r, fb_s, fb_r, turn_sem,
):
    here = lax.axis_index("expert")
    t = lax.axis_index("tensor")
    c = lax.axis_index("dp")
    y, z = here % N, here // N
    e = here // 2

    def ydev(k):
        return {"expert": z * N + (y + k + N) % N}

    def zdev(k):
        return {"expert": ((z + k + N) % N) * N + y}

    def xdev(k):
        return {"tensor": (t + k + X) % X}

    def copy(src, dst, ss, rs, dev):
        return pltpu.make_async_remote_copy(
            src_ref=src, dst_ref=dst, send_sem=ss, recv_sem=rs, device_id=dev, device_id_type=MESH
        )

    barrier = pltpu.get_barrier_semaphore()
    peers = [ydev(k) for k in range(1, N)] + [zdev(k) for k in range(1, N)]
    peers += [xdev(1), xdev(-1), xdev(2), {"dp": 1 - c}]
    for peer in peers:
        pl.semaphore_signal(barrier, inc=1, device_id=peer, device_id_type=MESH)

    local = [
        pltpu.make_async_copy(dw.at[0], WD, w_l.at[0]),
        pltpu.make_async_copy(gw.at[0, pl.ds(pl.multiple_of(t * 896, 128), 896)], WX.at[0, :, 0:128], w_l.at[1]),
        pltpu.make_async_copy(uw.at[0, pl.ds(pl.multiple_of(t * 896, 128), 896)], WX.at[0, :, 128:256], w_l.at[2]),
    ]
    first = pltpu.make_async_copy(tok_h, TOK, w_l.at[3])
    first.start()
    for d in local:
        d.start()
    AUX[0, 0] = gate_table(ids[...], gat[...])
    first.wait()
    block = dither_round(TOK[...], dit[...], t * TOK.shape[1])
    XA[0, 0] = block[:HALF]
    XB[0, 0] = block[HALF:]
    pl.semaphore_wait(barrier, len(peers))

    def dot(a, b):
        return jnp.dot(a, b, preferred_element_type=F32)

    def prepare(j):
        lane8, sub8 = iota((8, 128), 1), iota((8, 128), 0)
        pick = (sub8 % 4 == e // 8) & (lane8 // HALF == e % 8)
        packed = jnp.zeros((8, 128), F32)
        for k in range(N):
            w = jnp.where(pick, AUX[j, k], 0.0)
            packed = packed + (w if k == 0 else pltpu.roll(w, k * HALF, 1))
        packed = pltpu.roll(packed, ((8 - e % 8) % 8) * HALF, 1)
        g_a = jnp.sum(jnp.where(sub8 < 4, packed, 0.0), axis=0, keepdims=True)
        g_b = jnp.sum(jnp.where(sub8 >= 4, packed, 0.0), axis=0, keepdims=True)
        m_a, m_b = g_a > 0.0, g_b > 0.0
        marks = jnp.concatenate(
            [
                jnp.broadcast_to(jnp.where(m_a, 1.0, 0.0), (8, 128)),
                jnp.broadcast_to(jnp.where(m_b, 1.0, 0.0), (8, 128)),
            ],
            axis=0,
        ).astype(BF)
        r_i, l_i = iota((128, 128), 0), iota((128, 128), 1)
        same = r_i // HALF == l_i // HALF
        before = dot(marks, jnp.where(same & (r_i < l_i), 1.0, 0.0).astype(BF))
        whole = dot(marks, jnp.where(same, 1.0, 0.0).astype(BF))
        base = ((iota((1, 128), 1) // HALF) * HALF).astype(F32)
        code_a = jnp.where(m_a, base + before[0:1], -1.0)
        code_b = jnp.where(m_b, base + before[8:9] + whole[0:1], -1.0)
        row = r_i.astype(F32)
        p_a = jnp.where(code_a == row, 1.0, 0.0)
        p_b = jnp.where(code_b == row, 1.0, 0.0)
        GS[j] = jnp.sum(p_a * g_a + p_b * g_b, axis=1, keepdims=True)
        PT[j, 0:128] = p_a.T.astype(BF)
        PT[j, 128:256] = p_b.T.astype(BF)
        PP[j] = jnp.concatenate([p_a, p_b], axis=1).astype(BF)
    sent = []
    counter = [0]

    def go(src, dst, rs, dev):
        d = copy(src, dst, ag_s.at[counter[0]], ag_r.at[rs], dev)
        counter[0] += 1
        d.start()
        sent.append(d)

    def landed(ref, rs):
        pltpu.make_async_copy(ref, ref, ag_r.at[rs]).wait()

    A1, U1, B1 = 0, 8, 16
    A2, B2, U2 = 24, 40, 56

    def first_hop(k):
        h = k // 4
        go(XA.at[0, k], XA.at[1, k], A2 + 2 + h, zdev(1))
        go(XA.at[0, k], XA.at[7, k], A2 + 14 + h, zdev(-1))
        go(XB.at[0, k], XB.at[1, k], B2 + 2 + h, ydev(1))
        go(XB.at[0, k], XB.at[7, k], B2 + 14 + h, ydev(-1))

    def small_landed(k):
        landed(XA.at[0, k], A1 + k)
        landed(AUX.at[0, k], U1 + k)
        landed(XB.at[0, k], B1 + k)

    for k in NEAREST:
        go(XA.at[0, 0], XA.at[0, k], A1 + k, ydev(k))
        go(AUX.at[0, 0], AUX.at[0, k], U1 + k, ydev(k))
        go(XB.at[0, 0], XB.at[0, k], B1 + k, zdev(k))

    half = pl.multiple_of(c * 448, 64)
    wide = (slice(0, 128), slice(128, 256))

    def rows_for(k, start, size):
        return pl.ds(pl.multiple_of(((t + k + X) % X) * 896 + c * 448 + start, 32), size)

    near, far = [], []
    for p, w in enumerate((gw, uw)):
        near.append(copy(w.at[0, rows_for(1, 0, 448)], WX.at[3, pl.ds(half, 448), wide[p]], w_s.at[p], w_r.at[p], xdev(1)))
        near.append(copy(w.at[0, rows_for(-1, 0, 448)], WX.at[1, pl.ds(half, 448), wide[p]], w_s.at[2 + p], w_r.at[2 + p], xdev(-1)))
        far.append(copy(w.at[0, rows_for(2, 0, 224)], WF.at[0, :, wide[p]], w_s.at[4 + p], w_r.at[4 + p], xdev(1)))
        far.append(copy(w.at[0, rows_for(2, 224, 224)], WF.at[1, :, wide[p]], w_s.at[6 + p], w_r.at[6 + p], xdev(-1)))
    for d in far + near:
        d.start()
    lower = pl.ds(pl.multiple_of(c * 448, 32), 224)
    upper = pl.ds(pl.multiple_of(c * 448 + 224, 32), 224)
    onward = [
        copy(WF.at[0], WX.at[2, lower], w_s.at[8], w_r.at[8], xdev(1)),
        copy(WF.at[1], WX.at[2, upper], w_s.at[9], w_r.at[9], xdev(-1)),
    ]
    both = [
        copy(WX.at[r, pl.ds(half, 448)], WX.at[r, pl.ds(half, 448)], w_s.at[9 + r], w_r.at[9 + r], {"dp": 1 - c})
        for r in (1, 2, 3)
    ]

    def recut():
        for w in far:
            w.wait_recv()
        for w in onward:
            w.start()
        for w in near:
            w.wait_recv()
        both[0].start()
        both[2].start()

    def recut_end():
        for w in onward:
            w.wait_recv()
        both[1].start()

    if STAGGER:

        @pl.when(c == 1)
        def _():
            recut()
            recut_end()
            pl.semaphore_wait(turn_sem, 1)

    first_hop(0)
    for k in NEAREST:
        small_landed(k)
        first_hop(k)
    go(AUX.at[0], AUX.at[1], U2 + 1, zdev(1))
    go(AUX.at[0], AUX.at[7], U2 + 7, zdev(-1))

    for d in range(1, 4):
        for h in range(2):
            part = slice(4 * h, 4 * h + 4)
            for big, base, dev in ((XA, A2, zdev), (XB, B2, ydev)):
                landed(big.at[d, part], base + 2 * d + h)
                if d < 3 or h == 0:
                    go(big.at[d, part], big.at[d + 1, part], base + 2 * d + 2 + h, dev(1))
                landed(big.at[N - d, part], base + 2 * (N - d) + h)
                if d < 3 or h == 1:
                    go(big.at[N - d, part], big.at[N - d - 1, part], base + 2 * (N - d - 1) + h, dev(-1))
        landed(AUX.at[d], U2 + d)
        go(AUX.at[d], AUX.at[d + 1], U2 + d + 1, zdev(1))
        landed(AUX.at[N - d], U2 + N - d)
        if d < 3:
            go(AUX.at[N - d], AUX.at[N - d - 1], U2 + N - d - 1, zdev(-1))
        if d == 1:
            if STAGGER:
                pl.when(c == 0)(recut)
            else:
                recut()
            prepare(0)
        if d == 2:
            if STAGGER:
                pl.when(c == 0)(recut_end)
            else:
                recut_end()
        prepare(d)
        prepare(N - d)
    if STAGGER:

        @pl.when(c == 0)
        def _():
            pl.semaphore_signal(turn_sem, inc=1, device_id={"dp": 1 - c}, device_id_type=MESH)

    for h in range(2):
        part = slice(4 * h, 4 * h + 4)
        landed(XA.at[4, part], A2 + 8 + h)
        landed(XB.at[4, part], B2 + 8 + h)
    landed(AUX.at[4], U2 + 4)
    prepare(4)
    for d in local:
        d.wait()
    for d in both:
        d.wait_recv()

    mine = pl.ds(pl.multiple_of(t * 128, 128), 128)
    lo, hi = pl.ds(0, 64), pl.ds(64, 64)

    def xs(n, k):
        return x_s.at[n * 8 + k], x_r.at[n * 8 + k]

    def d_x(n):
        return [copy(SX.at[n, q], R2.at[n, q], *xs(n, q), xdev(k)) for q, k in enumerate((2, 1, -1))]

    def d_h(n):
        return [copy(HB.at[n, :, mine], HB.at[n, :, mine], *xs(n, 3 + q), xdev(k)) for q, k in enumerate((2, 1, -1))]

    def d_b(n, h):
        a, b = n * 8 + 2 * h, n * 8 + 2 * h + 1
        if h == 0:
            lefts, rights = (CB.at[n, 4, :, 0:CUT], RB.at[n, 3, :, 0:CUT]), (CB.at[n, 4, :, CUT:896], RB.at[n, 5, :, CUT:896])
        else:
            lefts, rights = (CB.at[n, 4 - h], RB.at[n, 3 - h]), (CB.at[n, 4 + h], RB.at[n, 5 + h])
        return [
            copy(*lefts, b_s.at[a], b_r.at[a], ydev(-1)),
            copy(*rights, b_s.at[b], b_r.at[b], ydev(1)),
        ]

    def d_fb(j):
        return copy(SB.at[j], FB.at[j], fb_s.at[j], fb_r.at[j], zdev(-j))

    def d_fa(k):
        return copy(SA.at[k], FA.at[k], fa_s.at[k], fa_r.at[k], ydev(-k))

    def d_ra0():
        return [
            copy(CA.at[0, lo], RA.at[3, lo], ra_s.at[0], ra_r.at[6], zdev(-1)),
            copy(CA.at[0, hi], RA.at[5, hi], ra_s.at[1], ra_r.at[11], zdev(1)),
        ]

    def d_ra_left(n, h):
        j = 4 - (n + 1) // 2
        part = (lo, hi)[h]
        return copy(CA.at[n, part], RA.at[j - 1, part], ra_s.at[2 * n + h], ra_r.at[2 * j - 2 + h], zdev(-1))

    def d_ra_right(n, h):
        j = 4 + n // 2
        part = (lo, hi)[h]
        return copy(CA.at[n, part], RA.at[j + 1, part], ra_s.at[2 * n + h], ra_r.at[2 * j + 2 + h], zdev(1))

    def ra_landed(ref, slot):
        pltpu.make_async_copy(ref, ref, ra_r.at[slot]).wait()

    def start(ds):
        for d in ds:
            d.start()

    def arrived(ds):
        for d in ds:
            d.wait_recv()

    def s0(n):
        j = group_of(n)
        rows = jnp.concatenate([XA[j].reshape(128, 896), XB[:, j].reshape(128, 896)], axis=0)
        routed = dot(PP[j], rows).astype(BF)
        for q, r in enumerate((2, 1, 3)):
            SX[n, q] = dot(routed, WX[r]).astype(BF)
            d_x(n)[q].start()
        OWN[n] = dot(routed, WX[0])

    def s2(n):
        arrived(d_x(n))
        pre = OWN[n] + R2[n, 0].astype(F32) + R2[n, 1].astype(F32) + R2[n, 2].astype(F32)
        gate, up = pre[:, 0:128], pre[:, 128:256]
        HB[n, :, mine] = (gate * jax.nn.sigmoid(gate) * up).astype(BF)
        start(d_h(n))

    def s4(n):
        arrived(d_h(n))
        j = group_of(n)
        result = (dot(HB[n], WD[...]) * GS[j]).astype(BF)
        back = dot(PT[j], result).astype(BF)
        CA[n] = back[0:128]
        CB[n] = back[128:256].reshape(8, HALF, 896)

        start(d_b(n, 0))

        @pl.when(n == 0)
        def _():
            start(d_ra0())

        @pl.when(n % 2 == 1)
        def _():
            j = 4 - (n + 1) // 2

            @pl.when(n < 7)
            def _():
                for h, part in enumerate((lo, hi)):
                    if h == 0:
                        ra_landed(RA.at[j, part], 2 * j + h)
                        CA[n, part] = CA[n, part] + RA[j, part]
                    else:

                        @pl.when(n > 1)
                        def _():
                            ra_landed(RA.at[j, part], 2 * j + h)
                            CA[n, part] = CA[n, part] + RA[j, part]

                    d_ra_left(n, h).start()

        @pl.when((n % 2 == 0) & (n > 0))
        def _():
            j = 4 + n // 2
            for h, part in ((1, hi), (0, lo)):
                if h == 1:
                    ra_landed(RA.at[j, part], 2 * j + h)
                    CA[n, part] = CA[n, part] + RA[j, part]
                else:

                    @pl.when(n > 2)
                    def _():
                        ra_landed(RA.at[j, part], 2 * j + h)
                        CA[n, part] = CA[n, part] + RA[j, part]

                d_ra_right(n, h).start()

        @pl.when(n == 7)
        def _():
            for h, part in enumerate((lo, hi)):
                ra_landed(RA.at[0, part], h)
                ra_landed(RA.at[8, part], 16 + h)
            for k in range(7, -1, -1):
                piece = pl.ds(k * HALF, HALF)
                total = CA[7, piece].astype(F32) + RA[0, piece].astype(F32) + RA[8, piece].astype(F32)
                if k == 0:
                    TA[...] = total
                else:
                    SA[k] = total.astype(BF)
                    d_fa(k).start()

    def s5(n, h):
        arrived(d_b(n, h - 1))
        if h == 1:
            CB[n, 3, :, 0:CUT] = CB[n, 3, :, 0:CUT] + RB[n, 3, :, 0:CUT]
            CB[n, 5, :, CUT:896] = CB[n, 5, :, CUT:896] + RB[n, 5, :, CUT:896]
        else:
            CB[n, 4 - h] = CB[n, 4 - h] + RB[n, 4 - h]
            CB[n, 4 + h] = CB[n, 4 + h] + RB[n, 4 + h]
        start(d_b(n, h))

    def s8(n):
        arrived(d_b(n, 3))
        j = group_of(n)
        total = CB[n, 0].astype(F32) + RB[n, 0].astype(F32) + RB[n, 8].astype(F32)

        @pl.when(n < 7)
        def _():
            SB[j] = total.astype(BF)
            d_fb(j).start()

        @pl.when(n == 7)
        def _():
            TB[...] = total

    last = 2 * LAG
    stages = [
        (last, 0, 8, s4),
        (last + 4 * HOP, 0, 8, s8),
        (last + 3 * HOP, 0, 8, functools.partial(s5, h=3)),
        (last + 2 * HOP, 0, 8, functools.partial(s5, h=2)),
        (last + 1 * HOP, 0, 8, functools.partial(s5, h=1)),
        (LAG, 0, 8, s2),
        (0, 0, 8, s0),
    ]
    turns = max(lag + to for lag, _, to, _ in stages)

    def turn(i, carry):
        for lag, since, to, stage in stages:

            @pl.when((i >= lag + since) & (i < lag + to))
            def _():
                stage(i - lag)

        return carry

    lax.fori_loop(0, turns, turn, 0)

    total_a, total_b = TA[...], TB[...]
    for k in range(1, N):
        d_fa(k).wait_recv()
        total_a = total_a + FA[k].astype(F32)
    for k in range(1, N):
        d_fb(k).wait_recv()
        total_b = total_b + FB[k].astype(F32)
    out[0:HALF] = total_a.astype(BF)
    out[HALF : 2 * HALF] = total_b.astype(BF)

    for d in sent + near + far + onward + both + d_ra0():
        d.wait_send()
    for h in range(2):
        for n in (1, 3, 5):
            d_ra_left(n, h).wait_send()
        for n in (2, 4, 6):
            d_ra_right(n, h).wait_send()

    def drain(n, carry):
        for d in d_x(n) + d_h(n):
            d.wait_send()

        for h in range(4):
            for d in d_b(n, h):
                d.wait_send()
        return carry

    lax.fori_loop(0, GROUPS, drain, 0)

    def drain_small(k, carry):
        d_fa(k).wait_send()
        d_fb(k).wait_send()
        return carry

    lax.fori_loop(1, N, drain_small, 0)


def on_device(tokens, dither, expert_ids, gate_values, gate_weight, up_weight, down_weight):
    rows, quarter = tokens.shape
    vmem = pl.BlockSpec(memory_space=pltpu.VMEM)
    hbm = pl.BlockSpec(memory_space=pl.ANY)
    dma = pltpu.SemaphoreType.DMA
    return pl.pallas_call(
        kernel,
        out_shape=jax.ShapeDtypeStruct((rows, quarter), BF),
        in_specs=[hbm] + [vmem] * 3 + [hbm] * 3,
        out_specs=vmem,
        scratch_shapes=[
            pltpu.VMEM((rows, quarter), BF),
            pltpu.VMEM((8, 128, 256), BF),
            pltpu.VMEM((8, 8, HALF, 896), BF),
            pltpu.VMEM((8, 8, HALF, 896), BF),
            pltpu.VMEM((8, 8, 8, 128), F32),
            pltpu.VMEM((4, 896, 256), BF),
            pltpu.VMEM((2, 224, 256), BF),
            pltpu.VMEM((512, 896), BF),
            pltpu.VMEM((8, 256, 128), BF),
            pltpu.VMEM((8, 128, 1), F32),
            pltpu.VMEM((8, 128, 256), F32),
            pltpu.VMEM((8, 3, 128, 256), BF),
            pltpu.VMEM((8, 3, 128, 256), BF),
            pltpu.VMEM((8, 128, 512), BF),
            pltpu.VMEM((8, 128, 896), BF),
            pltpu.VMEM((9, 128, 896), BF),
            pltpu.VMEM((8, 8, HALF, 896), BF),
            pltpu.VMEM((8, 9, HALF, 896), BF),
            pltpu.VMEM((8, HALF, 896), BF),
            pltpu.VMEM((8, HALF, 896), BF),
            pltpu.VMEM((8, HALF, 896), BF),
            pltpu.VMEM((8, HALF, 896), BF),
            pltpu.VMEM((HALF, 896), F32),
            pltpu.VMEM((HALF, 896), F32),
            dma((96,)),
            dma((64,)),
            dma((13,)),
            dma((13,)),
            dma((4,)),
            dma((64,)),
            dma((64,)),
            dma((16,)),
            dma((18,)),
            dma((64,)),
            dma((64,)),
            dma((8,)),
            dma((8,)),
            dma((8,)),
            dma((8,)),
            pltpu.SemaphoreType.REGULAR,
        ],
        compiler_params=pltpu.CompilerParams(
            collective_id=0, has_side_effects=True, vmem_limit_bytes=60 * 1024 * 1024
        ),
        cost_estimate=pl.CostEstimate(flops=5_000_000_000, bytes_accessed=4_000_000, transcendentals=200_000),
    )(tokens, dither.reshape(1, rows), expert_ids.T, gate_values.T, gate_weight, up_weight, down_weight)


def solution(mesh):
    in_specs = (
        P(("dp", "expert"), "tensor"),
        P(("dp", "expert")),
        P(("dp", "expert"), None),
        P(("dp", "expert"), None),
        P("expert", None, "tensor"),
        P("expert", None, "tensor"),
        P("expert", None, "tensor"),
    )
    return jax.shard_map(
        on_device, mesh=mesh, in_specs=in_specs, out_specs=P(("dp", "expert"), "tensor"), check_vma=False
    )
```

```python
import functools

import jax
import jax.numpy as jnp
from jax import lax
from jax.experimental import pallas as pl
from jax.experimental.pallas import tpu as pltpu
from jax.sharding import PartitionSpec as P

MESH = pl.DeviceIdType.MESH
BF = jnp.bfloat16
F32 = jnp.float32
N = 8
X = 4
HALF = 16
GROUPS = 8
CUT = 512
NEAREST = (1, 7, 2, 6, 3, 5, 4)
STAGGER = False
LAG = 2
HOP = 2


def iota(shape, axis):
    return lax.broadcasted_iota(jnp.int32, shape, axis)


def dither_round(values, dither_row, column_start):
    rows, cols = values.shape
    scaled = values.astype(F32)
    magnitude = jnp.abs(scaled)
    grid = jnp.full_like(scaled, 2.0**-26)
    inverse = jnp.full_like(scaled, 2.0**26)
    for octave in range(-23, 4):
        above = magnitude >= 2.0**octave
        grid = jnp.where(above, 2.0 ** (octave - 2), grid)
        inverse = jnp.where(above, 2.0 ** (2 - octave), inverse)
    square = jnp.broadcast_to(dither_row.astype(F32), (rows, rows))
    diagonal = iota((rows, rows), 0) == iota((rows, rows), 1)
    column = jnp.sum(jnp.where(diagonal, square, 0.0), axis=1, keepdims=True).astype(jnp.int32)
    offset = (column + 97 * (column_start + iota((rows, cols), 1))) & 255
    jitter = (offset.astype(F32) + 0.5) / 256.0
    return (jnp.floor(scaled * inverse + jitter) * grid).astype(BF)


def gate_table(ids, gates):
    rows = []
    expert = iota((8, 128), 1) // HALF
    for h in range(2):
        part = slice(h * HALF, h * HALF + HALF)
        wide_ids = jnp.concatenate([ids[:, part]] * 8, axis=1)
        wide_gates = jnp.concatenate([gates[:, part]] * 8, axis=1)
        for r in range(4):
            chosen = jnp.where(wide_ids == expert + 8 * r, wide_gates, 0.0)
            rows.append(jnp.sum(chosen, axis=0, keepdims=True))
    return jnp.concatenate(rows, axis=0)


def group_of(n):
    return jnp.where(n % 2 == 1, 4 - (n + 1) // 2, 4 + n // 2)


def kernel(
    tok_h, dit, ids, gat, gw, uw, dw, out,
    TOK, PP, XA, XB, AUX, WX, WF, WD, PT, GS, OWN, SX, R2, HB, CA, RA, CB, RB, FA, FB, SA, SB, TA, TB,
    ag_s, ag_r, w_s, w_r, w_l, x_s, x_r, ra_s, ra_r, b_s, b_r, fa_s, fa_r, fb_s, fb_r, turn_sem,
):
    here = lax.axis_index("expert")
    t = lax.axis_index("tensor")
    c = lax.axis_index("dp")
    y, z = here % N, here // N
    e = here // 2

    def ydev(k):
        return {"expert": z * N + (y + k + N) % N}

    def zdev(k):
        return {"expert": ((z + k + N) % N) * N + y}

    def xdev(k):
        return {"tensor": (t + k + X) % X}

    def copy(src, dst, ss, rs, dev):
        return pltpu.make_async_remote_copy(
            src_ref=src, dst_ref=dst, send_sem=ss, recv_sem=rs, device_id=dev, device_id_type=MESH
        )

    barrier = pltpu.get_barrier_semaphore()
    peers = [ydev(k) for k in range(1, N)] + [zdev(k) for k in range(1, N)]
    peers += [xdev(1), xdev(-1), xdev(2), {"dp": 1 - c}]
    for peer in peers:
        pl.semaphore_signal(barrier, inc=1, device_id=peer, device_id_type=MESH)

    local = [
        pltpu.make_async_copy(dw.at[0], WD, w_l.at[0]),
        pltpu.make_async_copy(gw.at[0, pl.ds(pl.multiple_of(t * 896, 128), 896)], WX.at[0, :, 0:128], w_l.at[1]),
        pltpu.make_async_copy(uw.at[0, pl.ds(pl.multiple_of(t * 896, 128), 896)], WX.at[0, :, 128:256], w_l.at[2]),
    ]
    first = pltpu.make_async_copy(tok_h, TOK, w_l.at[3])
    first.start()
    for d in local:
        d.start()
    AUX[0, 0] = gate_table(ids[...], gat[...])
    first.wait()
    block = dither_round(TOK[...], dit[...], t * TOK.shape[1])
    XA[0, 0] = block[:HALF]
    XB[0, 0] = block[HALF:]
    pl.semaphore_wait(barrier, len(peers))

    def dot(a, b):
        return jnp.dot(a, b, preferred_element_type=F32)

    def prepare(j):
        lane8, sub8 = iota((8, 128), 1), iota((8, 128), 0)
        pick = (sub8 % 4 == e // 8) & (lane8 // HALF == e % 8)
        packed = jnp.zeros((8, 128), F32)
        for k in range(N):
            w = jnp.where(pick, AUX[j, k], 0.0)
            packed = packed + (w if k == 0 else pltpu.roll(w, k * HALF, 1))
        packed = pltpu.roll(packed, ((8 - e % 8) % 8) * HALF, 1)
        g_a = jnp.sum(jnp.where(sub8 < 4, packed, 0.0), axis=0, keepdims=True)
        g_b = jnp.sum(jnp.where(sub8 >= 4, packed, 0.0), axis=0, keepdims=True)
        m_a, m_b = g_a > 0.0, g_b > 0.0
        marks = jnp.concatenate(
            [
                jnp.broadcast_to(jnp.where(m_a, 1.0, 0.0), (8, 128)),
                jnp.broadcast_to(jnp.where(m_b, 1.0, 0.0), (8, 128)),
            ],
            axis=0,
        ).astype(BF)
        r_i, l_i = iota((128, 128), 0), iota((128, 128), 1)
        same = r_i // HALF == l_i // HALF
        before = dot(marks, jnp.where(same & (r_i < l_i), 1.0, 0.0).astype(BF))
        whole = dot(marks, jnp.where(same, 1.0, 0.0).astype(BF))
        base = ((iota((1, 128), 1) // HALF) * HALF).astype(F32)
        code_a = jnp.where(m_a, base + before[0:1], -1.0)
        code_b = jnp.where(m_b, base + before[8:9] + whole[0:1], -1.0)
        row = r_i.astype(F32)
        p_a = jnp.where(code_a == row, 1.0, 0.0)
        p_b = jnp.where(code_b == row, 1.0, 0.0)
        GS[j] = jnp.sum(p_a * g_a + p_b * g_b, axis=1, keepdims=True)
        PT[j, 0:128] = p_a.T.astype(BF)
        PT[j, 128:256] = p_b.T.astype(BF)
        PP[j] = jnp.concatenate([p_a, p_b], axis=1).astype(BF)
    sent = []
    counter = [0]

    def go(src, dst, rs, dev):
        d = copy(src, dst, ag_s.at[counter[0]], ag_r.at[rs], dev)
        counter[0] += 1
        d.start()
        sent.append(d)

    def landed(ref, rs):
        pltpu.make_async_copy(ref, ref, ag_r.at[rs]).wait()

    A1, U1, B1 = 0, 8, 16
    A2, B2, U2 = 24, 40, 56

    def first_hop(k):
        h = k // 4
        go(XA.at[0, k], XA.at[1, k], A2 + 2 + h, zdev(1))
        go(XA.at[0, k], XA.at[7, k], A2 + 14 + h, zdev(-1))
        go(XB.at[0, k], XB.at[1, k], B2 + 2 + h, ydev(1))
        go(XB.at[0, k], XB.at[7, k], B2 + 14 + h, ydev(-1))

    def small_landed(k):
        landed(XA.at[0, k], A1 + k)
        landed(AUX.at[0, k], U1 + k)
        landed(XB.at[0, k], B1 + k)

    for k in NEAREST:
        go(XA.at[0, 0], XA.at[0, k], A1 + k, ydev(k))
        go(AUX.at[0, 0], AUX.at[0, k], U1 + k, ydev(k))
        go(XB.at[0, 0], XB.at[0, k], B1 + k, zdev(k))

    half = pl.multiple_of(c * 448, 64)
    wide = (slice(0, 128), slice(128, 256))

    def rows_for(k, start, size):
        return pl.ds(pl.multiple_of(((t + k + X) % X) * 896 + c * 448 + start, 32), size)

    near, far = [], []
    for p, w in enumerate((gw, uw)):
        near.append(copy(w.at[0, rows_for(1, 0, 448)], WX.at[3, pl.ds(half, 448), wide[p]], w_s.at[p], w_r.at[p], xdev(1)))
        near.append(copy(w.at[0, rows_for(-1, 0, 448)], WX.at[1, pl.ds(half, 448), wide[p]], w_s.at[2 + p], w_r.at[2 + p], xdev(-1)))
        far.append(copy(w.at[0, rows_for(2, 0, 224)], WF.at[0, :, wide[p]], w_s.at[4 + p], w_r.at[4 + p], xdev(1)))
        far.append(copy(w.at[0, rows_for(2, 224, 224)], WF.at[1, :, wide[p]], w_s.at[6 + p], w_r.at[6 + p], xdev(-1)))
    for d in far + near:
        d.start()
    lower = pl.ds(pl.multiple_of(c * 448, 32), 224)
    upper = pl.ds(pl.multiple_of(c * 448 + 224, 32), 224)
    onward = [
        copy(WF.at[0], WX.at[2, lower], w_s.at[8], w_r.at[8], xdev(1)),
        copy(WF.at[1], WX.at[2, upper], w_s.at[9], w_r.at[9], xdev(-1)),
    ]
    both = [
        copy(WX.at[r, pl.ds(half, 448)], WX.at[r, pl.ds(half, 448)], w_s.at[9 + r], w_r.at[9 + r], {"dp": 1 - c})
        for r in (1, 2, 3)
    ]

    def recut():
        for w in far:
            w.wait_recv()
        for w in onward:
            w.start()
        for w in near:
            w.wait_recv()
        both[0].start()
        both[2].start()

    def recut_end():
        for w in onward:
            w.wait_recv()
        both[1].start()

    if STAGGER:

        @pl.when(c == 1)
        def _():
            recut()
            recut_end()
            pl.semaphore_wait(turn_sem, 1)

    first_hop(0)
    for k in NEAREST:
        small_landed(k)
        first_hop(k)
    go(AUX.at[0], AUX.at[1], U2 + 1, zdev(1))
    go(AUX.at[0], AUX.at[7], U2 + 7, zdev(-1))

    for d in range(1, 4):
        for h in range(2):
            part = slice(4 * h, 4 * h + 4)
            for big, base, dev in ((XA, A2, zdev), (XB, B2, ydev)):
                landed(big.at[d, part], base + 2 * d + h)
                if d < 3 or h == 0:
                    go(big.at[d, part], big.at[d + 1, part], base + 2 * d + 2 + h, dev(1))
                landed(big.at[N - d, part], base + 2 * (N - d) + h)
                if d < 3 or h == 1:
                    go(big.at[N - d, part], big.at[N - d - 1, part], base + 2 * (N - d - 1) + h, dev(-1))
        landed(AUX.at[d], U2 + d)
        go(AUX.at[d], AUX.at[d + 1], U2 + d + 1, zdev(1))
        landed(AUX.at[N - d], U2 + N - d)
        if d < 3:
            go(AUX.at[N - d], AUX.at[N - d - 1], U2 + N - d - 1, zdev(-1))
        if d == 1:
            if STAGGER:
                pl.when(c == 0)(recut)
            else:
                recut()
            prepare(0)
        if d == 2:
            if STAGGER:
                pl.when(c == 0)(recut_end)
            else:
                recut_end()
        prepare(d)
        prepare(N - d)
    if STAGGER:

        @pl.when(c == 0)
        def _():
            pl.semaphore_signal(turn_sem, inc=1, device_id={"dp": 1 - c}, device_id_type=MESH)

    for h in range(2):
        part = slice(4 * h, 4 * h + 4)
        landed(XA.at[4, part], A2 + 8 + h)
        landed(XB.at[4, part], B2 + 8 + h)
    landed(AUX.at[4], U2 + 4)
    prepare(4)
    for d in local:
        d.wait()
    for d in both:
        d.wait_recv()

    mine = pl.ds(pl.multiple_of(t * 128, 128), 128)
    lo, hi = pl.ds(0, 64), pl.ds(64, 64)

    def xs(n, k):
        return x_s.at[n * 8 + k], x_r.at[n * 8 + k]

    def d_x(n):
        return [copy(SX.at[n, q], R2.at[n, q], *xs(n, q), xdev(k)) for q, k in enumerate((2, 1, -1))]

    def d_h(n):
        return [copy(HB.at[n, :, mine], HB.at[n, :, mine], *xs(n, 3 + q), xdev(k)) for q, k in enumerate((2, 1, -1))]

    def d_b(n, h):
        a, b = n * 8 + 2 * h, n * 8 + 2 * h + 1
        if h == 0:
            lefts, rights = (CB.at[n, 4, :, 0:CUT], RB.at[n, 3, :, 0:CUT]), (CB.at[n, 4, :, CUT:896], RB.at[n, 5, :, CUT:896])
        else:
            lefts, rights = (CB.at[n, 4 - h], RB.at[n, 3 - h]), (CB.at[n, 4 + h], RB.at[n, 5 + h])
        return [
            copy(*lefts, b_s.at[a], b_r.at[a], ydev(-1)),
            copy(*rights, b_s.at[b], b_r.at[b], ydev(1)),
        ]

    def d_fb(j):
        return copy(SB.at[j], FB.at[j], fb_s.at[j], fb_r.at[j], zdev(-j))

    def d_fa(k):
        return copy(SA.at[k], FA.at[k], fa_s.at[k], fa_r.at[k], ydev(-k))

    def d_ra0():
        return [
            copy(CA.at[0, lo], RA.at[3, lo], ra_s.at[0], ra_r.at[6], zdev(-1)),
            copy(CA.at[0, hi], RA.at[5, hi], ra_s.at[1], ra_r.at[11], zdev(1)),
        ]

    def d_ra_left(n, h):
        j = 4 - (n + 1) // 2
        part = (lo, hi)[h]
        return copy(CA.at[n, part], RA.at[j - 1, part], ra_s.at[2 * n + h], ra_r.at[2 * j - 2 + h], zdev(-1))

    def d_ra_right(n, h):
        j = 4 + n // 2
        part = (lo, hi)[h]
        return copy(CA.at[n, part], RA.at[j + 1, part], ra_s.at[2 * n + h], ra_r.at[2 * j + 2 + h], zdev(1))

    def ra_landed(ref, slot):
        pltpu.make_async_copy(ref, ref, ra_r.at[slot]).wait()

    def start(ds):
        for d in ds:
            d.start()

    def arrived(ds):
        for d in ds:
            d.wait_recv()

    def s0(n):
        j = group_of(n)
        rows = jnp.concatenate([XA[j].reshape(128, 896), XB[:, j].reshape(128, 896)], axis=0)
        routed = dot(PP[j], rows).astype(BF)
        for q, r in enumerate((2, 1, 3)):
            SX[n, q] = dot(routed, WX[r]).astype(BF)
            d_x(n)[q].start()
        OWN[n] = dot(routed, WX[0])

    def s2(n):
        arrived(d_x(n))
        pre = OWN[n] + R2[n, 0].astype(F32) + R2[n, 1].astype(F32) + R2[n, 2].astype(F32)
        gate, up = pre[:, 0:128], pre[:, 128:256]
        HB[n, :, mine] = (gate * jax.nn.sigmoid(gate) * up).astype(BF)
        start(d_h(n))

    def s4(n):
        arrived(d_h(n))
        j = group_of(n)
        result = (dot(HB[n], WD[...]) * GS[j]).astype(BF)
        back = dot(PT[j], result).astype(BF)
        CA[n] = back[0:128]
        CB[n] = back[128:256].reshape(8, HALF, 896)

        start(d_b(n, 0))

        @pl.when(n == 0)
        def _():
            start(d_ra0())

        @pl.when(n % 2 == 1)
        def _():
            j = 4 - (n + 1) // 2

            @pl.when(n < 7)
            def _():
                for h, part in enumerate((lo, hi)):
                    if h == 0:
                        ra_landed(RA.at[j, part], 2 * j + h)
                        CA[n, part] = CA[n, part] + RA[j, part]
                    else:

                        @pl.when(n > 1)
                        def _():
                            ra_landed(RA.at[j, part], 2 * j + h)
                            CA[n, part] = CA[n, part] + RA[j, part]

                    d_ra_left(n, h).start()

        @pl.when((n % 2 == 0) & (n > 0))
        def _():
            j = 4 + n // 2
            for h, part in ((1, hi), (0, lo)):
                if h == 1:
                    ra_landed(RA.at[j, part], 2 * j + h)
                    CA[n, part] = CA[n, part] + RA[j, part]
                else:

                    @pl.when(n > 2)
                    def _():
                        ra_landed(RA.at[j, part], 2 * j + h)
                        CA[n, part] = CA[n, part] + RA[j, part]

                d_ra_right(n, h).start()

        @pl.when(n == 7)
        def _():
            for h, part in enumerate((lo, hi)):
                ra_landed(RA.at[0, part], h)
                ra_landed(RA.at[8, part], 16 + h)
            for k in (4, 3, 5, 2, 6, 1, 7, 0):
                piece = pl.ds(k * HALF, HALF)
                total = CA[7, piece].astype(F32) + RA[0, piece].astype(F32) + RA[8, piece].astype(F32)
                if k == 0:
                    TA[...] = total
                else:
                    SA[k] = total.astype(BF)
                    d_fa(k).start()

    def s5(n, h):
        arrived(d_b(n, h - 1))
        if h == 1:
            CB[n, 3, :, 0:CUT] = CB[n, 3, :, 0:CUT] + RB[n, 3, :, 0:CUT]
            CB[n, 5, :, CUT:896] = CB[n, 5, :, CUT:896] + RB[n, 5, :, CUT:896]
        else:
            CB[n, 4 - h] = CB[n, 4 - h] + RB[n, 4 - h]
            CB[n, 4 + h] = CB[n, 4 + h] + RB[n, 4 + h]
        start(d_b(n, h))

    def s8(n):
        arrived(d_b(n, 3))
        j = group_of(n)
        total = CB[n, 0].astype(F32) + RB[n, 0].astype(F32) + RB[n, 8].astype(F32)

        @pl.when(n < 7)
        def _():
            SB[j] = total.astype(BF)
            d_fb(j).start()

        @pl.when(n == 7)
        def _():
            TB[...] = total

    last = 2 * LAG
    stages = [
        (last, 0, 8, s4),
        (last + 4 * HOP, 0, 8, s8),
        (last + 3 * HOP, 0, 8, functools.partial(s5, h=3)),
        (last + 2 * HOP, 0, 8, functools.partial(s5, h=2)),
        (last + 1 * HOP, 0, 8, functools.partial(s5, h=1)),
        (LAG, 0, 8, s2),
        (0, 0, 8, s0),
    ]
    turns = max(lag + to for lag, _, to, _ in stages)

    def turn(i, carry):
        for lag, since, to, stage in stages:

            @pl.when((i >= lag + since) & (i < lag + to))
            def _():
                stage(i - lag)

        return carry

    lax.fori_loop(0, turns, turn, 0)

    total_a, total_b = TA[...], TB[...]
    for k in range(1, N):
        d_fa(k).wait_recv()
        total_a = total_a + FA[k].astype(F32)
    for k in range(1, N):
        d_fb(k).wait_recv()
        total_b = total_b + FB[k].astype(F32)
    out[0:HALF] = total_a.astype(BF)
    out[HALF : 2 * HALF] = total_b.astype(BF)

    for d in sent + near + far + onward + both + d_ra0():
        d.wait_send()
    for h in range(2):
        for n in (1, 3, 5):
            d_ra_left(n, h).wait_send()
        for n in (2, 4, 6):
            d_ra_right(n, h).wait_send()

    def drain(n, carry):
        for d in d_x(n) + d_h(n):
            d.wait_send()

        for h in range(4):
            for d in d_b(n, h):
                d.wait_send()
        return carry

    lax.fori_loop(0, GROUPS, drain, 0)

    def drain_small(k, carry):
        d_fa(k).wait_send()
        d_fb(k).wait_send()
        return carry

    lax.fori_loop(1, N, drain_small, 0)


def on_device(tokens, dither, expert_ids, gate_values, gate_weight, up_weight, down_weight):
    rows, quarter = tokens.shape
    vmem = pl.BlockSpec(memory_space=pltpu.VMEM)
    hbm = pl.BlockSpec(memory_space=pl.ANY)
    dma = pltpu.SemaphoreType.DMA
    return pl.pallas_call(
        kernel,
        out_shape=jax.ShapeDtypeStruct((rows, quarter), BF),
        in_specs=[hbm] + [vmem] * 3 + [hbm] * 3,
        out_specs=vmem,
        scratch_shapes=[
            pltpu.VMEM((rows, quarter), BF),
            pltpu.VMEM((8, 128, 256), BF),
            pltpu.VMEM((8, 8, HALF, 896), BF),
            pltpu.VMEM((8, 8, HALF, 896), BF),
            pltpu.VMEM((8, 8, 8, 128), F32),
            pltpu.VMEM((4, 896, 256), BF),
            pltpu.VMEM((2, 224, 256), BF),
            pltpu.VMEM((512, 896), BF),
            pltpu.VMEM((8, 256, 128), BF),
            pltpu.VMEM((8, 128, 1), F32),
            pltpu.VMEM((8, 128, 256), F32),
            pltpu.VMEM((8, 3, 128, 256), BF),
            pltpu.VMEM((8, 3, 128, 256), BF),
            pltpu.VMEM((8, 128, 512), BF),
            pltpu.VMEM((8, 128, 896), BF),
            pltpu.VMEM((9, 128, 896), BF),
            pltpu.VMEM((8, 8, HALF, 896), BF),
            pltpu.VMEM((8, 9, HALF, 896), BF),
            pltpu.VMEM((8, HALF, 896), BF),
            pltpu.VMEM((8, HALF, 896), BF),
            pltpu.VMEM((8, HALF, 896), BF),
            pltpu.VMEM((8, HALF, 896), BF),
            pltpu.VMEM((HALF, 896), F32),
            pltpu.VMEM((HALF, 896), F32),
            dma((96,)),
            dma((64,)),
            dma((13,)),
            dma((13,)),
            dma((4,)),
            dma((64,)),
            dma((64,)),
            dma((16,)),
            dma((18,)),
            dma((64,)),
            dma((64,)),
            dma((8,)),
            dma((8,)),
            dma((8,)),
            dma((8,)),
            pltpu.SemaphoreType.REGULAR,
        ],
        compiler_params=pltpu.CompilerParams(
            collective_id=0, has_side_effects=True, vmem_limit_bytes=60 * 1024 * 1024
        ),
        cost_estimate=pl.CostEstimate(flops=5_000_000_000, bytes_accessed=4_000_000, transcendentals=200_000),
    )(tokens, dither.reshape(1, rows), expert_ids.T, gate_values.T, gate_weight, up_weight, down_weight)


def solution(mesh):
    in_specs = (
        P(("dp", "expert"), "tensor"),
        P(("dp", "expert")),
        P(("dp", "expert"), None),
        P(("dp", "expert"), None),
        P("expert", None, "tensor"),
        P("expert", None, "tensor"),
        P("expert", None, "tensor"),
    )
    return jax.shard_map(
        on_device, mesh=mesh, in_specs=in_specs, out_specs=P(("dp", "expert"), "tensor"), check_vma=False
    )
```
